32 devices in a mesh: layer: 2 (over core), row: 2 (over y), col: 8 (over z, x).
Axes of the slice: x: 2, y: 2, z: 4, core: 2. Of those that a mesh axis runs over, the one named last changes fastest.
Arguments:
- amplitudes: bfloat16 [64, 128, 128], P(('row', 'col')), may hold values from -6 to 6
- integrals: bfloat16 [4096, 128, 128], P(('layer', 'row', 'col')), may hold values from -0.1875 to 0.1875
- amp_index: int32 [512, 48], P(('layer', 'row', 'col')), may hold values from 0 to 7
- left_index: int32 [512, 48], P(('layer', 'row', 'col')), may hold values from 0 to 127, as said below
- right_index: int32 [512, 48], P(('layer', 'row', 'col')), may hold values from 0 to 127, as said below
- dest_col: int32 [256, 1], P(('row', 'col')), may hold values from 0 to 7; in each aligned block of 16 rows (0 to 15, 16 to 31, ...) at most 2 rows name the same one
- owner_slot: int32 [256], P(('row', 'col')), may hold values from 0 to 7
Outputs:
- ladder: float32 [128, 128, 128], P(('row', 'col'))
The draws below stay inside these ranges and needn't reach their ends.
Inputs may be any that keep to these rules, and one draw needn't show every extreme that they name: `dest_col`: among the 16 result tiles of one index of row and col, no owner column appears more than 2 times, and some column appears exactly 2 times. A term's amplitude tile is number amp_index among the tiles of the devices with the same col index, counted row by row. A term's left and right integral tiles belong to one auxiliary function: left_index // 2 == right_index // 2. right_index // 2 == left_index // 2 for every term.
All inputs are finite; a program needn't handle non-finite values.
Results may differ from the reference program's by a relative error of at most 0.0029.
Values may be sent and summed in bfloat16 or wider, within the bound.
No kernel may reach another device: no remote copies, remote signals or barrier semaphores. Data moves between devices by JAX's collectives and lax.ppermute only.
A program may use at most 64 MiB of HBM per device.

```python
import math
import jax
import jax.numpy as jnp
import numpy as np
from jax import lax

TILE = 128
AMP_DEV = 4
INTEGRAL_PER_GPU = 128
LOCAL = 16
TPR = 48
OWN = 8
CAP = 2
AMPLITUDE_COUNT = 64
INT_TILES = 4096
TASK_ROWS = 512
SLOTS = 256
N_LAYER = 2
N_ROW = 2
N_COL = 8


def term_tiles(key):
    base = jax.random.fold_in(key, 7331)
    aux_key = jax.random.fold_in(base, 1)
    side_key = jax.random.fold_in(base, 2)
    auxiliary = jax.random.randint(aux_key, (TASK_ROWS, TPR), 0, INTEGRAL_PER_GPU // 2, dtype=jnp.int32)
    sides = jax.random.randint(side_key, (2, TASK_ROWS, TPR), 0, 2, dtype=jnp.int32)
    left_tile_blocks = (2 * auxiliary + sides[0]).astype(jnp.int32)
    right_tiles = (2 * auxiliary + sides[1]).astype(jnp.int32)
    return (left_tile_blocks, right_tiles)


def draw_left_index(key, part):
    return term_tiles(key)[0]


def draw_right_index(key, part):
    return term_tiles(key)[1]


def plant(drawn, own_key, least, largest):
    spot = [jax.random.randint(jax.random.fold_in(own_key, axis), (), 0, length) for axis, length in enumerate(drawn.shape)]
    widest = drawn.shape.index(max(drawn.shape))
    next_to = spot[:widest] + [(spot[widest] + 1) % drawn.shape[widest]] + spot[widest + 1:]
    return drawn.at[tuple(spot)].set(least).at[tuple(next_to)].set(largest)


def level_of(stream_key, shape, shards, least, top_value):
    factor_of = 1.0
    for axis_at, parts in shards:
        heights = jax.random.uniform(jax.random.fold_in(jax.random.fold_in(stream_key, 6), axis_at), (parts,), jnp.float32, least / len(shards), top_value / len(shards))
        factor_of = factor_of * jnp.repeat(jnp.exp(heights), shape[axis_at] // parts).reshape((-1,) + (1,) * (len(shape) - 1 - axis_at))
    return factor_of


def deal_out(key, own, number, rows, count, top, reach, skew):
    ranking = jax.random.permutation(key, count)
    heavy_load, common = shares(count, rows * top, reach, skew, True), shares(count, rows * top, reach, skew, False)
    places = jnp.arange(count)

    def named(sizes, offset_by):
        used = int((sizes > 0).sum())
        fixed = max(1, used // 4)
        moved = fixed + (places - fixed + offset_by * (used - fixed)) % max(1, count - fixed)
        return jnp.zeros((count,), jnp.int32).at[ranking[jnp.where(places < fixed, places, moved)]].set(jnp.asarray(sizes, jnp.int32))

    sizes = jnp.where(number % 4 == 0, named(heavy_load, number // 4), named(common, number - number // 4 - 1))
    mixed = jax.random.permutation(jax.random.fold_in(own, 3), count)
    donor, taker = mixed[0:count // 2 * 2:2], mixed[1:count // 2 * 2:2]
    margin = jnp.minimum(sizes[donor] - 1, reach - sizes[taker]) // 2
    margin = jnp.where((donor == ranking[0]) | (taker == ranking[0]) | (sizes[taker] == 0), 0, jnp.maximum(margin, 0))
    moved = jax.random.randint(jax.random.fold_in(own, 4), (count // 2,), 0, 1 << 20) % (margin + 1)
    sizes = sizes.at[donor].add(-moved).at[taker].add(moved)
    members = jnp.searchsorted(jnp.cumsum(sizes), jnp.arange(rows * top), side="right").astype(jnp.int32)
    table = members.reshape(top, rows).T
    table = table[jax.random.permutation(jax.random.fold_in(own, 1), rows)]
    offset_by = jax.random.randint(jax.random.fold_in(own, 2), (rows, 1), 0, top)
    return jnp.take_along_axis(table, (jnp.arange(top)[None, :] + offset_by) % top, axis=1)


def shares(count, total, reach, lean, full):
    loads = [(1 << 20) // math.isqrt(rank ** lean) + 1 for rank in range(1, count + 1)]
    largest = reach if full else min(reach, max(-(-total // count), total * loads[0] // sum(loads)))
    least = 1 if total - largest >= count - 1 else 0
    given, spare = [largest] + [least] * (count - 1), total - largest - least * (count - 1)
    while spare > 0:
        candidates = [i for i in range(1, count) if given[i] < largest] or [i for i in range(1, count) if given[i] < reach]
        whole, remaining = sum([loads[i] for i in candidates]), spare
        for i in candidates:
            extra = min(reach - given[i], max(1, remaining * loads[i] // whole), spare)
            given[i] = given[i] + extra
            spare = spare - extra
    return np.array(given)


def bell_draw(rng, dims, deviation, reach, shards=(), kind=jnp.bfloat16):
    drawn = jax.random.normal(rng, dims, jnp.float32) * deviation
    if len(shards) > 0:
        drawn = level_of(rng, dims, shards, -0.22, 0.18) * drawn
    return jnp.clip(drawn, min=-reach, max=reach).astype(kind)


def setup_inputs(seed: int = 0) -> dict:
    seeds = jax.random.split(jax.random.key(seed), 8)
    amplitudes = bell_draw(seeds[0], (AMPLITUDE_COUNT, TILE, TILE), 1.0, 6.0, ((0, 16),))
    integrals = bell_draw(seeds[1], (INT_TILES, TILE, TILE), (8 * TILE) ** -0.5, 0.1875, ((0, 32),))
    amp_index = plant(jax.random.randint(seeds[2], (TASK_ROWS, TPR), 0, N_ROW * AMP_DEV), jax.random.fold_in(seeds[2], 1), 0, (N_ROW * AMP_DEV) - 1).astype(jnp.int32)
    left_index = draw_left_index(jax.random.fold_in(seeds[7], 71), 0)
    right_index = draw_right_index(jax.random.fold_in(seeds[7], 71), 0)
    dest_col_keys = jax.random.split(jax.random.fold_in(seeds[5], 1), SLOTS // LOCAL)
    dest_col_turns = jax.random.permutation(jax.random.fold_in(seeds[5], 3), SLOTS // LOCAL)
    dest_col = jax.vmap(lambda own, number: deal_out(jax.random.fold_in(seeds[5], 2), own, number, LOCAL, N_COL, 1, CAP, 2))(dest_col_keys, dest_col_turns).reshape((SLOTS, 1))
    owner_slot = plant(jax.random.randint(seeds[6], (SLOTS,), 0, OWN), jax.random.fold_in(seeds[6], 1), 0, OWN - 1).astype(jnp.int32)
    return dict(amplitudes=amplitudes, integrals=integrals, amp_index=amp_index, left_index=left_index, right_index=right_index, dest_col=dest_col, owner_slot=owner_slot)


def reference(amplitudes, integrals, amp_index, left_index, right_index, dest_col, owner_slot):
    groups = N_LAYER * N_ROW * N_COL

    def single_group(group):
        column = group % N_COL
        tiles = lax.dynamic_slice_in_dim(integrals, (group * INTEGRAL_PER_GPU).astype(jnp.int32), INTEGRAL_PER_GPU, 0)
        amp_rows = lax.dynamic_slice_in_dim(amp_index, (group * LOCAL).astype(jnp.int32), LOCAL, 0)
        left_rows = lax.dynamic_slice_in_dim(left_index, (group * LOCAL).astype(jnp.int32), LOCAL, 0)
        right_row_block = lax.dynamic_slice_in_dim(right_index, (group * LOCAL).astype(jnp.int32), LOCAL, 0)
        global_rows = (((amp_rows // AMP_DEV) * N_COL + column) * AMP_DEV + amp_rows % AMP_DEV).astype(jnp.int32)

        def one_slot(operand_list):
            amp_ids, left_ids, right_ids = operand_list
            amp_tiles = jnp.take(amplitudes, amp_ids, axis=0).astype(jnp.float32)
            right_tiles = jnp.take(tiles, right_ids, axis=0).astype(jnp.float32)
            middle_product = jnp.einsum('tcd,ted->tce', amp_tiles, right_tiles).astype(jnp.bfloat16)
            left_tile_blocks = jnp.take(tiles, left_ids, axis=0).astype(jnp.float32)
            return jnp.einsum('dov,dvh->oh', left_tile_blocks, middle_product.astype(jnp.float32))

        return lax.map(one_slot, (global_rows, left_rows, right_row_block))

    partials = lax.map(single_group, jnp.arange(groups, dtype=jnp.int32))
    partials = partials.reshape(N_LAYER, N_ROW * N_COL * LOCAL, TILE, TILE)
    slot_ids = jnp.arange(N_ROW * N_COL * LOCAL, dtype=jnp.int32)
    grid_row = slot_ids // (N_COL * LOCAL)
    target = ((grid_row * N_COL + dest_col[:, 0]) * OWN + owner_slot).astype(jnp.int32)
    ladder = jnp.zeros((N_ROW * N_COL * OWN, TILE, TILE), jnp.float32)
    for layer_id in range(N_LAYER):
        ladder = ladder.at[target].add(partials[layer_id])
    return ladder
```

```python
import functools

import jax
import jax.numpy as jnp
from jax import lax
from jax.experimental import pallas as pl
from jax.experimental.pallas import tpu as pltpu
from jax.sharding import PartitionSpec as P

OWN = 8
CAP = 2
LABEL_ROWS = 16
F32 = jnp.float32
BF16 = jnp.bfloat16
VMEM_BYTES = 56 << 20


def smem():
    return pl.BlockSpec(memory_space=pltpu.SMEM)


def vmem():
    return pl.BlockSpec(memory_space=pltpu.VMEM)


def transpose_kernel(tiles, flipped):
    count = tiles.shape[0]
    step = 8

    def body(i, carry):
        for j in range(step):
            flipped[i * step + j] = tiles[i * step + j].T
        return carry

    lax.fori_loop(0, count // step, body, 0)


def flip_tiles(integrals):
    return pl.pallas_call(
        transpose_kernel,
        out_shape=jax.ShapeDtypeStruct(integrals.shape, integrals.dtype),
        in_specs=[vmem()],
        out_specs=vmem(),
        compiler_params=pltpu.CompilerParams(vmem_limit_bytes=VMEM_BYTES),
        name="flip_tiles",
    )(integrals)


def ladder_kernel(
    columns, unroll, rank_of_layer, amp_ids, left_ids, right_ids, dest, labels, place,
    own_amp, other_amp, tiles, flipped, out, *rest,
):
    if len(rest) == 4:
        label_out, amps, slot_of, seen = rest
    else:
        label_out = None
        amps, slot_of, seen = rest
    slot_count, terms = amp_ids.shape
    amp_dev = own_amp.shape[0]
    layer = place[0]
    row = place[1]
    rank = layer if rank_of_layer else 1 - layer
    if other_amp is None:
        amps[...] = own_amp[...]
    else:
        amps[pl.ds(row * amp_dev, amp_dev)] = own_amp[...]
        amps[pl.ds((1 - row) * amp_dev, amp_dev)] = other_amp[...]
    for d in range(columns):
        slot_of[d] = 0
        seen[d] = 0

    def scan(k, carry):
        d = dest[k, 0]
        count = seen[d]
        seen[d] = count + 1

        @pl.when(count == rank)
        def _():
            slot_of[d] = k

        return carry

    lax.fori_loop(0, slot_count, scan, 0)

    def body(i, carry):
        for u in range(unroll):
            d = i * unroll + u
            k = slot_of[d]
            lefts = [tiles[left_ids[k, t]] for t in range(terms)]
            middles = [
                jnp.dot(
                    amps[amp_ids[k, t]], flipped[right_ids[k, t]], preferred_element_type=F32
                ).astype(BF16)
                for t in range(terms)
            ]
            out[d] = jnp.dot(
                jnp.concatenate(lefts, axis=1),
                jnp.concatenate(middles, axis=0),
                preferred_element_type=F32,
            )
            if label_out is not None:
                label = jnp.where(seen[d] > rank, labels[k], OWN).astype(F32)
                label_out[d] = jnp.full(label_out.shape[1:], label, F32).astype(BF16)
        return carry

    lax.fori_loop(0, columns // unroll, body, 0)


def owner_kernel(near, far, out):
    edge = out.shape[1]
    sources = near.shape[0]
    for chunk in range(edge // 32):
        rows = pl.ds(chunk * 32, 32)
        totals = [jnp.zeros((32, edge), F32) for _ in range(OWN)]
        for c in range(sources):
            for ref in (near, far):
                label = ref[c, edge : edge + LABEL_ROWS, :].astype(F32)
                label = jnp.concatenate([label] * (32 // LABEL_ROWS), axis=0)
                tile = ref[c, rows, :].astype(F32)
                for s in range(OWN):
                    totals[s] = totals[s] + jnp.where(label == s, tile, 0.0)
        for s in range(OWN):
            out[s, rows, :] = totals[s]


def swap(array, axis):
    size = lax.axis_size(axis)
    return lax.ppermute(array, axis, [(i, i ^ 1) for i in range(size)])


def shards(amplitudes, integrals, amp_index, left_index, right_index, dest_col, owner_slot):
    columns = lax.axis_size("col")
    rows = lax.axis_size("row")
    edge = integrals.shape[1]
    if rows == 2:
        amp_parts = (amplitudes, swap(amplitudes, "row"))
    else:
        amp_parts = (lax.all_gather(amplitudes, "row", axis=0, tiled=True),)
    amp_total = rows * amplitudes.shape[0]
    flipped = flip_tiles(integrals)
    place = jnp.stack([lax.axis_index("layer"), lax.axis_index("row")]).astype(jnp.int32)

    def ladder(keep):
        def kernel(*refs):
            head, tail = refs[:7], refs[7:]
            if rows != 2:
                tail = (None,) + tail
            return ladder_kernel(columns, 4, keep, *head, *tail)

        tile_out = jax.ShapeDtypeStruct((columns, edge, edge), F32)
        label_out = jax.ShapeDtypeStruct((columns, LABEL_ROWS, edge), BF16)
        return pl.pallas_call(
            kernel,
            out_shape=(tile_out, label_out) if keep else tile_out,
            in_specs=[smem()] * 6 + [vmem()] * (len(amp_parts) + 2),
            out_specs=(vmem(), vmem()) if keep else vmem(),
            scratch_shapes=[
                pltpu.VMEM((amp_total, edge, edge), BF16),
                pltpu.SMEM((columns,), jnp.int32),
                pltpu.SMEM((columns,), jnp.int32),
            ],
            cost_estimate=pl.CostEstimate(
                flops=columns * amp_index.shape[1] * 4 * edge**3, bytes_accessed=8 << 20, transcendentals=0
            ),
            compiler_params=pltpu.CompilerParams(vmem_limit_bytes=VMEM_BYTES),
            name="ladder_keep" if keep else "ladder_send",
        )(amp_index, left_index, right_index, dest_col, owner_slot, place, *amp_parts, integrals, flipped)

    sent = ladder(False)
    received = swap(sent, "layer")
    kept, labels = ladder(True)
    packed = jnp.concatenate([(kept + received).astype(BF16), labels], axis=1)
    near = lax.all_to_all(packed, "col", split_axis=0, concat_axis=0, tiled=True)
    far = swap(near, "layer")
    return pl.pallas_call(
        owner_kernel,
        out_shape=jax.ShapeDtypeStruct((OWN, edge, edge), F32),
        in_specs=[vmem(), vmem()],
        out_specs=vmem(),
        compiler_params=pltpu.CompilerParams(vmem_limit_bytes=VMEM_BYTES),
        name="owner_sum",
    )(near, far)


def solution(mesh):
    placed = (
        P(("row", "col"), None, None),
        P(("layer", "row", "col"), None, None),
        P(("layer", "row", "col"), None),
        P(("layer", "row", "col"), None),
        P(("layer", "row", "col"), None),
        P(("row", "col"), None),
        P(("row", "col")),
    )
    return jax.shard_map(
        shards, mesh=mesh, in_specs=placed, out_specs=P(("row", "col"), None, None), check_vma=False
    )
```

```python
import functools

import jax
import jax.numpy as jnp
from jax import lax
from jax.experimental import pallas as pl
from jax.experimental.pallas import tpu as pltpu
from jax.sharding import PartitionSpec as P

OWN = 8
CAP = 2
LABEL_ROWS = 16
F32 = jnp.float32
BF16 = jnp.bfloat16
VMEM_BYTES = 24 << 20


def smem():
    return pl.BlockSpec(memory_space=pltpu.SMEM)


def vmem():
    return pl.BlockSpec(memory_space=pltpu.VMEM)


def held(shape, dtype):
    return pltpu.VMEM(shape, dtype)


def in_vmem(array):
    return pltpu.with_memory_space_constraint(array, pltpu.VMEM)


def prepare_kernel(source, tiles, flipped, arrived):
    count = tiles.shape[0]
    chunks = arrived.shape[0]
    step = count // chunks

    def copy(i):
        span = pl.ds(i * step, step)
        return pltpu.make_async_copy(source.at[span], tiles.at[span], arrived.at[i])

    for i in range(chunks):
        copy(i).start()
    for i in range(chunks):
        copy(i).wait()

        def body(j, carry):
            for u in range(4):
                flipped[i * step + j * 4 + u] = tiles[i * step + j * 4 + u].T
            return carry

        lax.fori_loop(0, step // 4, body, 0)


def prepare(integrals):
    shape = integrals.shape
    return pl.pallas_call(
        prepare_kernel,
        out_shape=(held(shape, BF16), held(shape, BF16)),
        in_specs=[pl.BlockSpec(memory_space=pltpu.HBM)],
        out_specs=(vmem(), vmem()),
        scratch_shapes=[pltpu.SemaphoreType.DMA((8,))],
        compiler_params=pltpu.CompilerParams(vmem_limit_bytes=VMEM_BYTES),
        name="load_and_flip",
    )(pltpu.with_memory_space_constraint(integrals, pltpu.HBM))


def ladder_kernel(
    columns, unroll, rank_of_layer, amp_ids, left_ids, right_ids, dest, labels, own_amp, other_amp,
    tiles, flipped, out, *rest,
):
    if len(rest) == 4:
        label_out, amps, slot_of, seen = rest
    else:
        label_out = None
        amps, slot_of, seen = rest
    slot_count, terms = amp_ids.shape
    amp_dev = own_amp.shape[0]
    layer = lax.axis_index("layer")
    row = lax.axis_index("row")
    rank = layer if rank_of_layer else 1 - layer
    if other_amp is None:
        amps[...] = own_amp[...]
    else:
        amps[pl.ds(row * amp_dev, amp_dev)] = own_amp[...]
        amps[pl.ds((1 - row) * amp_dev, amp_dev)] = other_amp[...]
    for d in range(columns):
        slot_of[d] = 0
        seen[d] = 0

    def scan(k, carry):
        d = dest[k]
        count = seen[d]
        seen[d] = count + 1

        @pl.when(count == rank)
        def _():
            slot_of[d] = k

        return carry

    lax.fori_loop(0, slot_count, scan, 0)

    def body(i, carry):
        for u in range(unroll):
            d = i * unroll + u
            k = slot_of[d]
            lefts = [tiles[left_ids[k, t]] for t in range(terms)]
            middles = [
                jnp.dot(
                    amps[amp_ids[k, t]], flipped[right_ids[k, t]], preferred_element_type=F32
                ).astype(BF16)
                for t in range(terms)
            ]
            out[d] = jnp.dot(
                jnp.concatenate(lefts, axis=1),
                jnp.concatenate(middles, axis=0),
                preferred_element_type=F32,
            )
            if label_out is not None:
                label = jnp.where(seen[d] > rank, labels[k], OWN).astype(F32)
                label_out[d] = jnp.full(label_out.shape[1:], label, F32).astype(BF16)
        return carry

    lax.fori_loop(0, columns // unroll, body, 0)


def owner_kernel(near, far, out):
    edge = out.shape[1]
    sources = near.shape[0]
    for chunk in range(edge // 32):
        rows = pl.ds(chunk * 32, 32)
        totals = [jnp.zeros((32, edge), F32) for _ in range(OWN)]
        for c in range(sources):
            for ref in (near, far):
                label = ref[c, edge : edge + LABEL_ROWS, :].astype(F32)
                label = jnp.concatenate([label] * (32 // LABEL_ROWS), axis=0)
                tile = ref[c, rows, :].astype(F32)
                for s in range(OWN):
                    totals[s] = totals[s] + jnp.where(label == s, tile, 0.0)
        for s in range(OWN):
            out[s, rows, :] = totals[s]


def merge_kernel(kept, received, labels, packed):
    edge = kept.shape[1]
    for c in range(kept.shape[0]):
        packed[c, :edge] = (kept[c] + received[c]).astype(BF16)
        packed[c, edge:] = labels[c]


def swap(array, axis):
    size = lax.axis_size(axis)
    return lax.ppermute(array, axis, [(i, i ^ 1) for i in range(size)])


def shards(amplitudes, integrals, amp_index, left_index, right_index, dest_col, owner_slot):
    columns = lax.axis_size("col")
    rows = lax.axis_size("row")
    edge = integrals.shape[1]
    if rows == 2:
        amp_parts = (amplitudes, swap(amplitudes, "row"))
    else:
        amp_parts = (lax.all_gather(amplitudes, "row", axis=0, tiled=True),)
    amp_total = rows * amplitudes.shape[0]
    tiles, flipped = prepare(integrals)
    params = pltpu.CompilerParams(vmem_limit_bytes=VMEM_BYTES)
    target = dest_col.reshape(-1)

    def ladder(keep):
        def kernel(*refs):
            head, tail = refs[:6], refs[6:]
            if rows != 2:
                tail = (None,) + tail
            return ladder_kernel(columns, 4, keep, *head, *tail)

        tile_out = held((columns, edge, edge), F32)
        label_out = held((columns, LABEL_ROWS, edge), BF16)
        return pl.pallas_call(
            kernel,
            out_shape=(tile_out, label_out) if keep else tile_out,
            in_specs=[smem()] * 5 + [vmem()] * (len(amp_parts) + 2),
            out_specs=(vmem(), vmem()) if keep else vmem(),
            scratch_shapes=[
                pltpu.VMEM((amp_total, edge, edge), BF16),
                pltpu.SMEM((columns,), jnp.int32),
                pltpu.SMEM((columns,), jnp.int32),
            ],
            cost_estimate=pl.CostEstimate(
                flops=columns * amp_index.shape[1] * 4 * edge**3, bytes_accessed=1 << 20, transcendentals=0
            ),
            compiler_params=params,
            name="ladder_keep" if keep else "ladder_send",
        )(
            amp_index, left_index, right_index, target, owner_slot,
            *[in_vmem(part) for part in amp_parts], in_vmem(tiles), in_vmem(flipped),
        )

    sent = ladder(False)
    received = swap(sent, "layer")
    kept, labels = ladder(True)
    packed = pl.pallas_call(
        merge_kernel,
        out_shape=held((columns, edge + LABEL_ROWS, edge), BF16),
        in_specs=[vmem()] * 3,
        out_specs=vmem(),
        compiler_params=params,
        name="merge_layers",
    )(in_vmem(kept), in_vmem(received), in_vmem(labels))
    near = lax.all_to_all(packed, "col", split_axis=0, concat_axis=0, tiled=True)
    far = swap(near, "layer")
    return pl.pallas_call(
        owner_kernel,
        out_shape=jax.ShapeDtypeStruct((OWN, edge, edge), F32),
        in_specs=[vmem(), vmem()],
        out_specs=vmem(),
        compiler_params=params,
        name="owner_sum",
    )(in_vmem(near), in_vmem(far))


def solution(mesh):
    placed = (
        P(("row", "col"), None, None),
        P(("layer", "row", "col"), None, None),
        P(("layer", "row", "col"), None),
        P(("layer", "row", "col"), None),
        P(("layer", "row", "col"), None),
        P(("row", "col"), None),
        P(("row", "col")),
    )
    return jax.shard_map(
        shards, mesh=mesh, in_specs=placed, out_specs=P(("row", "col"), None, None), check_vma=False
    )
```

```python
import functools

import jax
import jax.numpy as jnp
from jax import lax
from jax.experimental import pallas as pl
from jax.experimental.pallas import tpu as pltpu
from jax.sharding import PartitionSpec as P

OWN = 8
CAP = 2
LABEL_ROWS = 8
F32 = jnp.float32
BF16 = jnp.bfloat16
VMEM_BYTES = 24 << 20


def smem():
    return pl.BlockSpec(memory_space=pltpu.SMEM)


def vmem():
    return pl.BlockSpec(memory_space=pltpu.VMEM)


def held(shape, dtype):
    return pltpu.VMEM(shape, dtype)


def in_vmem(array):
    return pltpu.with_memory_space_constraint(array, pltpu.VMEM)


def params():
    return pltpu.CompilerParams(vmem_limit_bytes=VMEM_BYTES)


def exchange_rounds(columns):
    far = list(range(columns - 1, 3, -1))
    pairs = [(far[i], far[i + 1]) for i in range(0, len(far), 2)]
    return pairs + [(3, 0), (1, 2)]


def prepare_kernel(
    bits, source, amp_ids, left_ids, right_ids, dest, labels,
    tiles, flipped, table, label_blocks, packed, seen, arrived,
):
    count = tiles.shape[0]
    chunks = arrived.shape[0]
    step = count // chunks
    columns = label_blocks.shape[0]

    def copy(i):
        span = pl.ds(i * step, step)
        return pltpu.make_async_copy(source.at[span], tiles.at[span], arrived.at[i])

    for i in range(chunks):
        copy(i).start()

    packed[...] = (amp_ids[...] << (2 * bits)) | (left_ids[...] << bits) | right_ids[...]
    table[...] = jnp.zeros(table.shape, jnp.int32)
    label_blocks[...] = jnp.full(label_blocks.shape, OWN, F32)
    for d in range(columns):
        seen[d] = 0
    me = lax.axis_index("col")
    for k in range(packed.shape[0]):
        offset = dest[k] ^ me
        rank = seen[offset]
        seen[offset] = rank + 1
        table[pl.ds(offset * CAP + rank, 1), :] = packed[pl.ds(k, 1), :]
        spot = pl.ds(pl.multiple_of(rank * LABEL_ROWS, LABEL_ROWS), LABEL_ROWS)
        label_blocks[offset, spot, :] = jnp.full((LABEL_ROWS, label_blocks.shape[2]), labels[k].astype(F32))

    for i in range(chunks):
        copy(i).wait()
        for j in range(step):
            flipped[i * step + j] = tiles[i * step + j].T


def prepare(columns, bits, integrals, amp_index, left_index, right_index, target, owner_slot):
    shape = integrals.shape
    slots, terms = amp_index.shape
    return pl.pallas_call(
        functools.partial(prepare_kernel, bits),
        out_shape=(
            held(shape, BF16),
            held(shape, BF16),
            held((columns * CAP, terms), jnp.int32),
            held((columns, CAP * LABEL_ROWS, shape[2]), F32),
        ),
        in_specs=[pl.BlockSpec(memory_space=pltpu.HBM)] + [vmem()] * 3 + [smem()] * 2,
        out_specs=(vmem(),) * 4,
        scratch_shapes=[
            pltpu.VMEM((slots, terms), jnp.int32),
            pltpu.SMEM((columns,), jnp.int32),
            pltpu.SemaphoreType.DMA((8,)),
        ],
        compiler_params=params(),
        name="load_and_flip",
    )(
        pltpu.with_memory_space_constraint(integrals, pltpu.HBM),
        in_vmem(amp_index), in_vmem(left_index), in_vmem(right_index), target, owner_slot,
    )


def pick(pair, layer):
    return jnp.where(layer == 0, pair[0], pair[1])


def ladder_kernel(bits, keeps, sends, parts, waits, *refs):
    table = refs[0]
    amp_parts = refs[1 : 1 + parts]
    tiles, flipped = refs[1 + parts : 3 + parts]
    outs, amps = refs[3 + parts + waits : -1], refs[-1]
    terms = table.shape[1]
    layer = lax.axis_index("layer")
    amp_dev = amp_parts[0].shape[0]
    if parts == 1:
        amps[...] = amp_parts[0][...]
    else:
        row = lax.axis_index("row")
        amps[pl.ds(row * amp_dev, amp_dev)] = amp_parts[0][...]
        amps[pl.ds((1 - row) * amp_dev, amp_dev)] = amp_parts[1][...]
    mask = (1 << bits) - 1
    picked = [(outs[0], i, pick(pair, layer)) for i, pair in enumerate(keeps)]
    picked += [(outs[-1], i, pick(pair, 1 - layer)) for i, pair in enumerate(sends)]
    for out, i, offset in picked:
        for rank in range(CAP):
            slot = offset * CAP + rank
            lefts, middles = [], []
            for t in range(terms):
                word = table[slot, t]
                lefts.append(tiles[(word >> bits) & mask])
                middles.append(
                    jnp.dot(
                        amps[word >> (2 * bits)], flipped[word & mask], preferred_element_type=F32
                    ).astype(BF16)
                )
            out[i * CAP + rank] = jnp.dot(
                jnp.concatenate(lefts, axis=1),
                jnp.concatenate(middles, axis=0),
                preferred_element_type=F32,
            )


def merge_kernel(pair, kept, received, label_blocks, packed):
    edge = kept.shape[1]
    for rank in range(CAP):
        packed[rank * edge : (rank + 1) * edge] = (kept[rank] + received[rank]).astype(BF16)
    packed[CAP * edge :] = label_blocks[pick(pair, lax.axis_index("layer"))].astype(BF16)


def owner_kernel(count, *refs):
    packs, out = refs[:count], refs[-1]
    base = refs[count] if len(refs) == count + 2 else None
    edge = out.shape[1]
    height = 32
    for chunk in range(edge // height):
        rows = pl.ds(chunk * height, height)
        totals = [jnp.zeros((height, edge), F32) if base is None else base[s, rows, :] for s in range(OWN)]
        for pack in packs:
            marks = pack[CAP * edge : CAP * (edge + LABEL_ROWS), :].astype(F32)
            for rank in range(CAP):
                mark = marks[rank * LABEL_ROWS : (rank + 1) * LABEL_ROWS]
                mark = jnp.concatenate([mark] * (height // LABEL_ROWS), axis=0)
                tile = pack[pl.ds(rank * edge + chunk * height, height), :].astype(F32)
                for s in range(OWN):
                    totals[s] = totals[s] + jnp.where(mark == s, tile, 0.0)
        for s in range(OWN):
            out[s, rows, :] = totals[s]


def swap(array, axis):
    size = lax.axis_size(axis)
    return lax.ppermute(array, axis, [(i, i ^ 1) for i in range(size)])


def shards(amplitudes, integrals, amp_index, left_index, right_index, dest_col, owner_slot):
    columns = lax.axis_size("col")
    rows = lax.axis_size("row")
    edge = integrals.shape[1]
    bits = (integrals.shape[0] - 1).bit_length()
    if rows == 2:
        amp_parts = (amplitudes, swap(amplitudes, "row"))
    else:
        amp_parts = (lax.all_gather(amplitudes, "row", axis=0, tiled=True),)
    amp_total = rows * amplitudes.shape[0]
    tiles, flipped, table, label_blocks = prepare(
        columns, bits, integrals, amp_index, left_index, right_index, dest_col.reshape(-1), owner_slot
    )
    rounds = exchange_rounds(columns)

    def ladder(keeps, sends, after):
        groups = [len(group) * CAP for group in (keeps, sends) if group]
        return pl.pallas_call(
            functools.partial(ladder_kernel, bits, keeps, sends, len(amp_parts), len(after)),
            out_shape=tuple(held((slots, edge, edge), F32) for slots in groups),
            in_specs=[smem()] + [vmem()] * (len(amp_parts) + 2) + [pl.BlockSpec(memory_space=pl.ANY)] * len(after),
            out_specs=(vmem(),) * len(groups),
            scratch_shapes=[pltpu.VMEM((amp_total, edge, edge), BF16)],
            cost_estimate=pl.CostEstimate(
                flops=sum(groups) * table.shape[1] * 4 * edge**3, bytes_accessed=1 << 20, transcendentals=0
            ),
            compiler_params=params(),
            name="ladder",
        )(table, *[in_vmem(part) for part in amp_parts], in_vmem(tiles), in_vmem(flipped), *after)

    def merge(pair, kept, received):
        return pl.pallas_call(
            functools.partial(merge_kernel, pair),
            out_shape=held((CAP * (edge + LABEL_ROWS), edge), BF16),
            in_specs=[vmem()] * 3,
            out_specs=vmem(),
            compiler_params=params(),
            name="merge_layers",
        )(in_vmem(kept), in_vmem(received), in_vmem(label_blocks))

    def deliver(pair, pack):
        route = [
            (layer * columns + c, layer * columns + (c ^ pair[layer])) for layer in range(2) for c in range(columns)
        ]
        near = lax.ppermute(pack, ("layer", "col"), route)
        return near, swap(near, "layer")

    def owner_sum(packs, base, shape):
        extra = () if base is None else (base,)
        return pl.pallas_call(
            functools.partial(owner_kernel, len(packs)),
            out_shape=shape,
            in_specs=[vmem()] * (len(packs) + len(extra)),
            out_specs=vmem(),
            compiler_params=params(),
            name="owner_sum",
        )(*[in_vmem(pack) for pack in packs], *[in_vmem(array) for array in extra])

    packs = []
    after = []
    (sent,) = ladder([], rounds[:1], after)
    received = swap(sent, "layer")
    for i, pair in enumerate(rounds):
        nexts = rounds[i + 1 : i + 2]
        kept, *sent = ladder([pair], nexts, after)
        pack = merge(pair, kept, received)
        if nexts:
            received = swap(sent[0], "layer")
        after = [pack] + [both[0] for both in packs[-1:]]
        packs.append(deliver(pair, pack))
    early = [pack for both in packs[:-1] for pack in both]
    base = owner_sum(early, None, held((OWN, edge, edge), F32))
    return owner_sum(list(packs[-1]), base, jax.ShapeDtypeStruct((OWN, edge, edge), F32))


def solution(mesh):
    placed = (
        P(("row", "col"), None, None),
        P(("layer", "row", "col"), None, None),
        P(("layer", "row", "col"), None),
        P(("layer", "row", "col"), None),
        P(("layer", "row", "col"), None),
        P(("row", "col"), None),
        P(("row", "col")),
    )
    return jax.shard_map(
        shards, mesh=mesh, in_specs=placed, out_specs=P(("row", "col"), None, None), check_vma=False
    )
```

```python
import functools

import jax
import jax.numpy as jnp
from jax import lax
from jax.experimental import pallas as pl
from jax.experimental.pallas import tpu as pltpu
from jax.sharding import PartitionSpec as P

OWN = 8
CAP = 2
LABEL_ROWS = 8
F32 = jnp.float32
BF16 = jnp.bfloat16
VMEM_BYTES = 24 << 20


def smem():
    return pl.BlockSpec(memory_space=pltpu.SMEM)


def vmem():
    return pl.BlockSpec(memory_space=pltpu.VMEM)


def held(shape, dtype):
    return pltpu.VMEM(shape, dtype)


def in_vmem(array):
    return pltpu.with_memory_space_constraint(array, pltpu.VMEM)


def params():
    return pltpu.CompilerParams(vmem_limit_bytes=VMEM_BYTES)


def exchange_rounds(columns):
    far = list(range(columns - 1, 3, -1))
    pairs = [(far[i], far[i + 1]) for i in range(0, len(far), 2)]
    return pairs + [(2, 3), (1, 0)]


def prepare_kernel(
    bits, source, amp_ids, left_ids, right_ids, dest_in, labels_in,
    tiles, flipped, table, label_blocks, ids, packed, dest, labels, seen, arrived, ready,
):
    count = tiles.shape[0]
    chunks = arrived.shape[0]
    step = count // chunks
    columns = label_blocks.shape[0]
    small = [
        pltpu.make_async_copy(src, dst, ready.at[i])
        for i, (src, dst) in enumerate(
            [(dest_in, dest), (labels_in, labels)]
            + [(src, ids.at[i]) for i, src in enumerate((amp_ids, left_ids, right_ids))]
        )
    ]

    def copy(i):
        span = pl.ds(i * step, step)
        return pltpu.make_async_copy(source.at[span], tiles.at[span], arrived.at[i])

    for transfer in small:
        transfer.start()
    for i in range(chunks):
        copy(i).start()

    table[...] = jnp.zeros(table.shape, jnp.int32)
    label_blocks[...] = jnp.full(label_blocks.shape, OWN, F32)
    for d in range(columns):
        seen[d] = 0
    me = lax.axis_index("col")
    for transfer in small:
        transfer.wait()
    packed[...] = (ids[0] << (2 * bits)) | (ids[1] << bits) | ids[2]
    for k in range(packed.shape[0]):
        offset = dest[k] ^ me
        rank = seen[offset]
        seen[offset] = rank + 1
        table[pl.ds(offset * CAP + rank, 1), :] = packed[pl.ds(k, 1), :]
        spot = pl.ds(pl.multiple_of(rank * LABEL_ROWS, LABEL_ROWS), LABEL_ROWS)
        label_blocks[offset, spot, :] = jnp.full((LABEL_ROWS, label_blocks.shape[2]), labels[k].astype(F32))

    for i in range(chunks):
        copy(i).wait()
        for j in range(step):
            flipped[i * step + j] = tiles[i * step + j].T


def prepare(columns, bits, integrals, amp_index, left_index, right_index, target, owner_slot):
    shape = integrals.shape
    slots, terms = amp_index.shape
    operands = (integrals, amp_index, left_index, right_index, target, owner_slot)
    return pl.pallas_call(
        functools.partial(prepare_kernel, bits),
        out_shape=(
            held(shape, BF16),
            held(shape, BF16),
            held((columns * CAP, terms), jnp.int32),
            held((columns, CAP * LABEL_ROWS, shape[2]), F32),
        ),
        in_specs=[pl.BlockSpec(memory_space=pltpu.HBM)] * len(operands),
        out_specs=(vmem(),) * 4,
        scratch_shapes=[
            pltpu.VMEM((3, slots, terms), jnp.int32),
            pltpu.VMEM((slots, terms), jnp.int32),
            pltpu.SMEM((slots,), jnp.int32),
            pltpu.SMEM((slots,), jnp.int32),
            pltpu.SMEM((columns,), jnp.int32),
            pltpu.SemaphoreType.DMA((8,)),
            pltpu.SemaphoreType.DMA((5,)),
        ],
        compiler_params=params(),
        name="load_and_flip",
    )(*[pltpu.with_memory_space_constraint(array, pltpu.HBM) for array in operands])


def pick(pair, layer):
    return jnp.where(layer == 0, pair[0], pair[1])


def ladder_kernel(bits, keeps, sends, parts, waits, *refs):
    table = refs[0]
    amp_parts = refs[1 : 1 + parts]
    tiles, flipped = refs[1 + parts : 3 + parts]
    outs, amps = refs[3 + parts + waits : -1], refs[-1]
    terms = table.shape[1]
    layer = lax.axis_index("layer")
    amp_dev = amp_parts[0].shape[0]
    if parts == 1:
        amps[...] = amp_parts[0][...]
    else:
        row = lax.axis_index("row")
        amps[pl.ds(row * amp_dev, amp_dev)] = amp_parts[0][...]
        amps[pl.ds((1 - row) * amp_dev, amp_dev)] = amp_parts[1][...]
    mask = (1 << bits) - 1
    picked = [(outs[0], i, pick(pair, layer)) for i, pair in enumerate(keeps)]
    picked += [(outs[-1], i, pick(pair, 1 - layer)) for i, pair in enumerate(sends)]
    for out, i, offset in picked:
        for rank in range(CAP):
            slot = offset * CAP + rank
            lefts, middles = [], []
            for t in range(terms):
                word = table[slot, t]
                lefts.append(tiles[(word >> bits) & mask])
                middles.append(
                    jnp.dot(
                        amps[word >> (2 * bits)], flipped[word & mask], preferred_element_type=F32
                    ).astype(BF16)
                )
            out[i * CAP + rank] = jnp.dot(
                jnp.concatenate(lefts, axis=1),
                jnp.concatenate(middles, axis=0),
                preferred_element_type=F32,
            )


def merge_kernel(pairs, first, kept, received, label_blocks, *packs):
    edge = kept.shape[1]
    layer = lax.axis_index("layer")
    for i, (pair, packed) in enumerate(zip(pairs, packs)):
        for rank in range(CAP):
            total = kept[i * CAP + rank] + received[(first + i) * CAP + rank]
            packed[rank * edge : (rank + 1) * edge] = total.astype(BF16)
        packed[CAP * edge :] = label_blocks[pick(pair, layer)].astype(BF16)


def owner_kernel(count, *refs):
    packs, out = refs[:count], refs[-1]
    base = refs[count] if len(refs) == count + 2 else None
    edge = out.shape[1]
    height = 32
    for chunk in range(edge // height):
        rows = pl.ds(chunk * height, height)
        totals = [jnp.zeros((height, edge), F32) if base is None else base[s, rows, :] for s in range(OWN)]
        for pack in packs:
            marks = pack[CAP * edge : CAP * (edge + LABEL_ROWS), :].astype(F32)
            for rank in range(CAP):
                mark = marks[rank * LABEL_ROWS : (rank + 1) * LABEL_ROWS]
                mark = jnp.concatenate([mark] * (height // LABEL_ROWS), axis=0)
                tile = pack[pl.ds(rank * edge + chunk * height, height), :].astype(F32)
                for s in range(OWN):
                    totals[s] = totals[s] + jnp.where(mark == s, tile, 0.0)
        for s in range(OWN):
            out[s, rows, :] = totals[s]


def swap(array, axis):
    size = lax.axis_size(axis)
    return lax.ppermute(array, axis, [(i, i ^ 1) for i in range(size)])


def shards(amplitudes, integrals, amp_index, left_index, right_index, dest_col, owner_slot):
    columns = lax.axis_size("col")
    rows = lax.axis_size("row")
    edge = integrals.shape[1]
    bits = (integrals.shape[0] - 1).bit_length()
    if rows == 2:
        amp_parts = (amplitudes, swap(amplitudes, "row"))
    else:
        amp_parts = (lax.all_gather(amplitudes, "row", axis=0, tiled=True),)
    amp_total = rows * amplitudes.shape[0]
    tiles, flipped, table, label_blocks = prepare(
        columns, bits, integrals, amp_index, left_index, right_index, dest_col.reshape(-1), owner_slot
    )
    rounds = exchange_rounds(columns)

    def ladder(keeps, sends, after):
        groups = [len(group) * CAP for group in (keeps, sends) if group]
        return pl.pallas_call(
            functools.partial(ladder_kernel, bits, keeps, sends, len(amp_parts), len(after)),
            out_shape=tuple(held((slots, edge, edge), F32) for slots in groups),
            in_specs=[smem()] + [vmem()] * (len(amp_parts) + 2) + [pl.BlockSpec(memory_space=pl.ANY)] * len(after),
            out_specs=(vmem(),) * len(groups),
            scratch_shapes=[pltpu.VMEM((amp_total, edge, edge), BF16)],
            cost_estimate=pl.CostEstimate(
                flops=sum(groups) * table.shape[1] * 4 * edge**3, bytes_accessed=1 << 20, transcendentals=0
            ),
            compiler_params=params(),
            name="ladder",
        )(table, *[in_vmem(part) for part in amp_parts], in_vmem(tiles), in_vmem(flipped), *after)

    def merge(pairs, first, kept, received):
        pack = held((CAP * (edge + LABEL_ROWS), edge), BF16)
        return pl.pallas_call(
            functools.partial(merge_kernel, pairs, first),
            out_shape=(pack,) * len(pairs),
            in_specs=[vmem()] * 3,
            out_specs=(vmem(),) * len(pairs),
            compiler_params=params(),
            name="merge_layers",
        )(in_vmem(kept), in_vmem(received), in_vmem(label_blocks))

    def send(pair, pack, cross):
        route = [
            (layer * columns + c, (layer ^ cross) * columns + (c ^ pair[layer]))
            for layer in range(2)
            for c in range(columns)
        ]
        return lax.ppermute(pack, ("layer", "col"), route)

    def owner_sum(packs, base, shape):
        extra = () if base is None else (base,)
        return pl.pallas_call(
            functools.partial(owner_kernel, len(packs)),
            out_shape=shape,
            in_specs=[vmem()] * (len(packs) + len(extra)),
            out_specs=vmem(),
            cost_estimate=pl.CostEstimate(flops=1 << 24, bytes_accessed=4 << 20, transcendentals=0),
            compiler_params=params(),
            name="owner_sum",
        )(*[in_vmem(pack) for pack in packs], *[in_vmem(array) for array in extra])

    stages = [rounds[:-2], rounds[-2:]]
    (sent,) = ladder([], rounds, [])
    received = swap(sent, "layer")
    near, far = [], []
    first, after = 0, []
    for pairs in stages:
        (kept,) = ladder(pairs, [], after)
        after = merge(pairs, first, kept, received)
        for pair, pack in zip(pairs, after):
            near.append(send(pair, pack, 0))
            far.append(send(pair, pack, 1) if pair == rounds[-1] else swap(near[-1], "layer"))
        first += len(pairs)
    count = len(stages[0])
    base = owner_sum(near[:count] + far[:count], None, held((OWN, edge, edge), F32))
    return owner_sum(near[count:] + far[count:], base, jax.ShapeDtypeStruct((OWN, edge, edge), F32))


def solution(mesh):
    placed = (
        P(("row", "col"), None, None),
        P(("layer", "row", "col"), None, None),
        P(("layer", "row", "col"), None),
        P(("layer", "row", "col"), None),
        P(("layer", "row", "col"), None),
        P(("row", "col"), None),
        P(("row", "col")),
    )
    return jax.shard_map(
        shards, mesh=mesh, in_specs=placed, out_specs=P(("row", "col"), None, None), check_vma=False
    )
```

```python
import functools

import jax
import jax.numpy as jnp
from jax import lax
from jax.experimental import pallas as pl
from jax.experimental.pallas import tpu as pltpu
from jax.sharding import PartitionSpec as P

OWN = 8
CAP = 2
LABEL_ROWS = 8
F32 = jnp.float32
BF16 = jnp.bfloat16
VMEM_BYTES = 24 << 20


def smem():
    return pl.BlockSpec(memory_space=pltpu.SMEM)


def vmem():
    return pl.BlockSpec(memory_space=pltpu.VMEM)


def held(shape, dtype):
    return pltpu.VMEM(shape, dtype)


def in_vmem(array):
    return pltpu.with_memory_space_constraint(array, pltpu.VMEM)


def params():
    return pltpu.CompilerParams(vmem_limit_bytes=VMEM_BYTES)


def brief():
    return pl.CostEstimate(flops=1 << 20, bytes_accessed=1 << 10, transcendentals=0)


def exchange_rounds(columns):
    far = list(range(columns - 1, 3, -1))
    pairs = [(far[i], far[i + 1]) for i in range(0, len(far), 2)]
    return pairs + [(0, 3), (1, 2)]


def prepare_kernel(
    bits, source, amp_ids, left_ids, right_ids, dest_in, labels_in,
    tiles, flipped, table, label_blocks, ids, packed, sorted_ids, dest, labels, seen, arrived, ready,
):
    count = tiles.shape[0]
    chunks = arrived.shape[0]
    step = count // chunks
    columns = label_blocks.shape[0]
    small = [
        pltpu.make_async_copy(src, dst, ready.at[i])
        for i, (src, dst) in enumerate(
            [(dest_in, dest), (labels_in, labels)]
            + [(src, ids.at[i]) for i, src in enumerate((amp_ids, left_ids, right_ids))]
        )
    ]

    def copy(i):
        span = pl.ds(i * step, step)
        return pltpu.make_async_copy(source.at[span], tiles.at[span], arrived.at[i])

    for transfer in small:
        transfer.start()
    for i in range(chunks):
        copy(i).start()

    sorted_ids[...] = jnp.zeros(sorted_ids.shape, jnp.int32)
    label_blocks[...] = jnp.full(label_blocks.shape, OWN, F32)
    for d in range(columns):
        seen[d] = 0

    def flip(i):
        copy(i).wait()
        for j in range(step):
            flipped[i * step + j] = tiles[i * step + j].T

    for i in range(chunks // 2):
        flip(i)

    me = lax.axis_index("col")
    for transfer in small:
        transfer.wait()
    packed[...] = (ids[0] << (2 * bits)) | (ids[1] << bits) | ids[2]
    for k in range(packed.shape[0]):
        offset = dest[k] ^ me
        rank = seen[offset]
        seen[offset] = rank + 1
        sorted_ids[pl.ds(offset * CAP + rank, 1), :] = packed[pl.ds(k, 1), :]
        spot = pl.ds(pl.multiple_of(rank * LABEL_ROWS, LABEL_ROWS), LABEL_ROWS)
        label_blocks[offset, spot, :] = jnp.full((LABEL_ROWS, label_blocks.shape[2]), labels[k].astype(F32))
    publish = pltpu.make_async_copy(sorted_ids, table, ready.at[len(small)])
    publish.start()

    for i in range(chunks // 2, chunks):
        flip(i)
    publish.wait()


def prepare(columns, bits, integrals, amp_index, left_index, right_index, target, owner_slot):
    shape = integrals.shape
    slots, terms = amp_index.shape
    operands = (integrals, amp_index, left_index, right_index, target, owner_slot)
    return pl.pallas_call(
        functools.partial(prepare_kernel, bits),
        out_shape=(
            held(shape, BF16),
            held(shape, BF16),
            pltpu.SMEM((columns * CAP, terms), jnp.int32),
            held((columns, CAP * LABEL_ROWS, shape[2]), F32),
        ),
        in_specs=[pl.BlockSpec(memory_space=pltpu.HBM)] * len(operands),
        out_specs=(vmem(), vmem(), smem(), vmem()),
        scratch_shapes=[
            pltpu.VMEM((3, slots, terms), jnp.int32),
            pltpu.VMEM((slots, terms), jnp.int32),
            pltpu.VMEM((columns * CAP, terms), jnp.int32),
            pltpu.SMEM((slots,), jnp.int32),
            pltpu.SMEM((slots,), jnp.int32),
            pltpu.SMEM((columns,), jnp.int32),
            pltpu.SemaphoreType.DMA((8,)),
            pltpu.SemaphoreType.DMA((6,)),
        ],
        cost_estimate=brief(),
        compiler_params=params(),
        name="load_and_flip",
    )(*[pltpu.with_memory_space_constraint(array, pltpu.HBM) for array in operands])


def pick(pair, layer):
    return jnp.where(layer == 0, pair[0], pair[1])


def ladder_kernel(bits, keeps, sends, parts, waits, *refs):
    table = refs[0]
    amp_parts = refs[1 : 1 + parts]
    tiles, flipped = refs[1 + parts : 3 + parts]
    outs, amps = refs[3 + parts + waits : -1], refs[-1]
    terms = table.shape[1]
    layer = lax.axis_index("layer")
    amp_dev = amp_parts[0].shape[0]
    if parts == 1:
        amps[...] = amp_parts[0][...]
    else:
        row = lax.axis_index("row")
        amps[pl.ds(row * amp_dev, amp_dev)] = amp_parts[0][...]
        amps[pl.ds((1 - row) * amp_dev, amp_dev)] = amp_parts[1][...]
    mask = (1 << bits) - 1
    picked = [(outs[0], i, pick(pair, layer)) for i, pair in enumerate(keeps)]
    picked += [(outs[-1], i, pick(pair, 1 - layer)) for i, pair in enumerate(sends)]
    for out, i, offset in picked:
        for rank in range(CAP):
            slot = offset * CAP + rank
            lefts, middles = [], []
            for t in range(terms):
                word = table[slot, t]
                lefts.append(tiles[(word >> bits) & mask])
                middles.append(
                    jnp.dot(
                        amps[word >> (2 * bits)], flipped[word & mask], preferred_element_type=F32
                    ).astype(BF16)
                )
            out[i * CAP + rank] = jnp.dot(
                jnp.concatenate(lefts, axis=1),
                jnp.concatenate(middles, axis=0),
                preferred_element_type=F32,
            ).astype(out.dtype)


def merge_kernel(pairs, skip, kept, received, label_blocks, *packs):
    edge = kept.shape[1]
    layer = lax.axis_index("layer")
    for i, (pair, packed) in enumerate(zip(pairs, packs)):
        for rank in range(CAP):
            tile = i * CAP + rank
            other = received[tile] if skip is None else received[skip + tile * edge : skip + (tile + 1) * edge]
            packed[rank * edge : (rank + 1) * edge] = (kept[tile] + other.astype(F32)).astype(BF16)
        packed[CAP * edge :] = label_blocks[pick(pair, layer)].astype(BF16)


def join_kernel(*refs):
    packs, sent, joined = refs[:-2], refs[-2], refs[-1]
    start = 0
    for part in [*packs, *[sent.at[i] for i in range(sent.shape[0])]]:
        joined[start : start + part.shape[0]] = part[...]
        start += part.shape[0]


def late_join_kernel(local_layer, own, middle, last, joined):
    joined[0] = jnp.where(lax.axis_index("layer") == local_layer, own[...], middle[...])
    joined[1] = last[...]


def pieces(packs, rows, edge):
    for pack in packs:
        marks = pack[CAP * edge : CAP * (edge + LABEL_ROWS), :].astype(F32)
        for rank in range(CAP):
            mark = marks[rank * LABEL_ROWS : (rank + 1) * LABEL_ROWS].reshape(1, LABEL_ROWS, edge)
            tile = pack[pl.ds(rank * edge + rows.start, rows.size), :].astype(F32)
            yield mark, tile.reshape(rows.size // LABEL_ROWS, LABEL_ROWS, edge)


def add_owned(total, parts, s):
    for mark, tile in parts:
        term = jnp.where(mark == s, tile, 0.0)
        total = term if total is None else total + term
    return total


def early_owner_kernel(count, near, far, out):
    edge = out.shape[2]
    size = CAP * (edge + LABEL_ROWS)

    def packs(ref):
        return [ref.at[pl.ds(i * size, size)] for i in range(count)]

    for start in range(0, edge, 32):
        rows = pl.ds(start, 32)
        sides = [list(pieces(packs(ref), rows, edge)) for ref in (near, far)]
        for s in range(OWN):
            total = add_owned(None, sides[0], s) + add_owned(None, sides[1], s)
            out[s, rows, :] = total.reshape(32, edge)


def last_owner_kernel(base, near, far, out, total, sent):
    edge = out.shape[2]
    chunks = sent.shape[0]
    height = edge // chunks

    def copy(i):
        rows = pl.ds(i * height, height)
        return pltpu.make_async_copy(total.at[:, rows, :], out.at[:, rows, :], sent.at[i])

    for i in range(chunks):
        rows = pl.ds(i * height, height)
        sides = [list(pieces([ref.at[k] for k in range(ref.shape[0])], rows, edge)) for ref in (near, far)]
        for s in range(OWN):
            late = add_owned(None, sides[0], s) + add_owned(None, sides[1], s)
            total[s, rows, :] = base[s, rows, :] + late.reshape(height, edge)
        copy(i).start()
    for i in range(chunks):
        copy(i).wait()


def swap(array, axis):
    size = lax.axis_size(axis)
    return lax.ppermute(array, axis, [(i, i ^ 1) for i in range(size)])


def shards(amplitudes, integrals, amp_index, left_index, right_index, dest_col, owner_slot):
    columns = lax.axis_size("col")
    rows = lax.axis_size("row")
    edge = integrals.shape[1]
    bits = (integrals.shape[0] - 1).bit_length()
    if rows == 2:
        amp_parts = (amplitudes, swap(amplitudes, "row"))
    else:
        amp_parts = (lax.all_gather(amplitudes, "row", axis=0, tiled=True),)
    amp_total = rows * amplitudes.shape[0]
    tiles, flipped, table, label_blocks = prepare(
        columns, bits, integrals, amp_index, left_index, right_index, dest_col.reshape(-1), owner_slot
    )
    rounds = exchange_rounds(columns)

    def ladder(keeps, sends, after, sent_type=F32):
        groups = [(len(group) * CAP, kind) for group, kind in ((keeps, F32), (sends, sent_type)) if group]
        return pl.pallas_call(
            functools.partial(ladder_kernel, bits, keeps, sends, len(amp_parts), len(after)),
            out_shape=tuple(held((slots, edge, edge), kind) for slots, kind in groups),
            in_specs=[smem()] + [vmem()] * (len(amp_parts) + 2) + [pl.BlockSpec(memory_space=pl.ANY)] * len(after),
            out_specs=(vmem(),) * len(groups),
            scratch_shapes=[pltpu.VMEM((amp_total, edge, edge), BF16)],
            cost_estimate=brief(),
            compiler_params=params(),
            name="ladder",
        )(pltpu.with_memory_space_constraint(table, pltpu.SMEM), *[in_vmem(part) for part in amp_parts], in_vmem(tiles), in_vmem(flipped), *after)

    pack_shape = (CAP * (edge + LABEL_ROWS), edge)

    def merge(pairs, skip, kept, received):
        return pl.pallas_call(
            functools.partial(merge_kernel, pairs, skip),
            out_shape=(held(pack_shape, BF16),) * len(pairs),
            in_specs=[vmem()] * 3,
            out_specs=(vmem(),) * len(pairs),
            cost_estimate=brief(),
            compiler_params=params(),
            name="merge_layers",
        )(in_vmem(kept), in_vmem(received), in_vmem(label_blocks))

    def join(packs, sent):
        rows = len(packs) * pack_shape[0] + sent.shape[0] * edge
        return pl.pallas_call(
            join_kernel,
            out_shape=held((rows, edge), BF16),
            in_specs=[vmem()] * (len(packs) + 1),
            out_specs=vmem(),
            cost_estimate=brief(),
            compiler_params=params(),
            name="join_packs",
        )(*[in_vmem(pack) for pack in packs], in_vmem(sent))

    def late_join(*packs):
        return pl.pallas_call(
            functools.partial(late_join_kernel, late[0].index(0)),
            out_shape=held((2, *pack_shape), BF16),
            in_specs=[vmem()] * len(packs),
            out_specs=vmem(),
            cost_estimate=brief(),
            compiler_params=params(),
            name="join_late_packs",
        )(*[in_vmem(pack) for pack in packs])

    def send(pair, pack, cross):
        route = [
            (layer * columns + c, (layer ^ cross) * columns + (c ^ pair[layer]))
            for layer in range(2)
            for c in range(columns)
            if pair[layer]
        ]
        return lax.ppermute(pack, ("layer", "col"), route)

    owned = (OWN, edge, edge)

    def early_owner_sum(near, far):
        return pl.pallas_call(
            functools.partial(early_owner_kernel, len(early)),
            out_shape=held(owned, F32),
            in_specs=[vmem()] * 2,
            out_specs=vmem(),
            cost_estimate=brief(),
            compiler_params=params(),
            name="early_owner_sum",
        )(in_vmem(near), in_vmem(far))

    def last_owner_sum(*arrays):
        return pl.pallas_call(
            last_owner_kernel,
            out_shape=jax.ShapeDtypeStruct(owned, F32),
            in_specs=[vmem()] * len(arrays),
            out_specs=pl.BlockSpec(memory_space=pl.ANY),
            scratch_shapes=[pltpu.VMEM(owned, F32), pltpu.SemaphoreType.DMA((4,))],
            cost_estimate=brief(),
            compiler_params=params(),
            name="last_owner_sum",
        )(*[in_vmem(array) for array in arrays])

    early, late = rounds[:-2], rounds[-2:]
    (sent,) = ladder([], early, [])
    received = swap(sent, "layer")
    (kept,) = ladder(early, [], [sent])
    packs = merge(early, None, kept, received)
    near = [send(pair, pack, 0) for pair, pack in zip(early, packs)]

    kept, sent = ladder(late, late, packs, BF16)
    joined = join(near, sent)
    far_joined = swap(joined, "layer")
    packs = merge(late, len(near) * pack_shape[0], kept, far_joined)
    middle, last = [send(pair, pack, 0) for pair, pack in zip(late, packs)]
    base = early_owner_sum(joined, far_joined)
    near = late_join(packs[0], middle, last)
    return last_owner_sum(base, near, swap(near, "layer"))


def solution(mesh):
    placed = (
        P(("row", "col"), None, None),
        P(("layer", "row", "col"), None, None),
        P(("layer", "row", "col"), None),
        P(("layer", "row", "col"), None),
        P(("layer", "row", "col"), None),
        P(("row", "col"), None),
        P(("row", "col")),
    )
    return jax.shard_map(
        shards, mesh=mesh, in_specs=placed, out_specs=P(("row", "col"), None, None), check_vma=False
    )
```

```python
import functools

import jax
import jax.numpy as jnp
from jax import lax
from jax.experimental import pallas as pl
from jax.experimental.pallas import tpu as pltpu
from jax.sharding import PartitionSpec as P

OWN = 8
CAP = 2
LABEL_ROWS = 8
F32 = jnp.float32
BF16 = jnp.bfloat16
VMEM_BYTES = 24 << 20


def smem():
    return pl.BlockSpec(memory_space=pltpu.SMEM)


def vmem():
    return pl.BlockSpec(memory_space=pltpu.VMEM)


def held(shape, dtype):
    return pltpu.VMEM(shape, dtype)


def in_vmem(array):
    return pltpu.with_memory_space_constraint(array, pltpu.VMEM)


def params():
    return pltpu.CompilerParams(vmem_limit_bytes=VMEM_BYTES)


def brief():
    return pl.CostEstimate(flops=1 << 20, bytes_accessed=1 << 10, transcendentals=0)


def round_slots(pair):
    return [tuple(offset * CAP + rank for offset in pair) for rank in range(CAP)]


def late_slots():
    return [tuple(offset * CAP + rank for rank in range(CAP)) for offset in (1, 0)]


def prepare_kernel(
    bits, source, amp_ids, left_ids, right_ids, dest_in, labels_in,
    tiles, flipped, table, label_blocks, ids, packed, sorted_ids, dest, labels, seen, arrived, ready,
):
    count = tiles.shape[0]
    chunks = arrived.shape[0]
    step = count // chunks
    columns = label_blocks.shape[0]
    small = [
        pltpu.make_async_copy(src, dst, ready.at[i])
        for i, (src, dst) in enumerate(
            [(dest_in, dest), (labels_in, labels)]
            + [(src, ids.at[i]) for i, src in enumerate((amp_ids, left_ids, right_ids))]
        )
    ]

    def copy(i):
        span = pl.ds(i * step, step)
        return pltpu.make_async_copy(source.at[span], tiles.at[span], arrived.at[i])

    for transfer in small:
        transfer.start()
    for i in range(chunks):
        copy(i).start()

    sorted_ids[...] = jnp.zeros(sorted_ids.shape, jnp.int32)
    label_blocks[...] = jnp.full(label_blocks.shape, OWN, F32)
    for d in range(columns):
        seen[d] = 0

    def flip(i):
        copy(i).wait()
        for j in range(step):
            flipped[i * step + j] = tiles[i * step + j].T

    for i in range(chunks // 2):
        flip(i)

    me = lax.axis_index("col")
    for transfer in small:
        transfer.wait()
    packed[...] = (ids[0] << (2 * bits)) | (ids[1] << bits) | ids[2]
    for k in range(packed.shape[0]):
        offset = dest[k] ^ me
        rank = seen[offset]
        seen[offset] = rank + 1
        sorted_ids[pl.ds(offset * CAP + rank, 1), :] = packed[pl.ds(k, 1), :]
        spot = pl.ds(pl.multiple_of(rank * LABEL_ROWS, LABEL_ROWS), LABEL_ROWS)
        label_blocks[offset, spot, :] = jnp.full((LABEL_ROWS, label_blocks.shape[2]), labels[k].astype(F32))
    publish = pltpu.make_async_copy(sorted_ids, table, ready.at[len(small)])
    publish.start()

    for i in range(chunks // 2, chunks):
        flip(i)
    publish.wait()


def prepare(columns, bits, integrals, amp_index, left_index, right_index, target, owner_slot):
    shape = integrals.shape
    slots, terms = amp_index.shape
    operands = (integrals, amp_index, left_index, right_index, target, owner_slot)
    return pl.pallas_call(
        functools.partial(prepare_kernel, bits),
        out_shape=(
            held(shape, BF16),
            held(shape, BF16),
            pltpu.SMEM((columns * CAP, terms), jnp.int32),
            held((columns, CAP * LABEL_ROWS, shape[2]), F32),
        ),
        in_specs=[pl.BlockSpec(memory_space=pltpu.HBM)] * len(operands),
        out_specs=(vmem(), vmem(), smem(), vmem()),
        scratch_shapes=[
            pltpu.VMEM((3, slots, terms), jnp.int32),
            pltpu.VMEM((slots, terms), jnp.int32),
            pltpu.VMEM((columns * CAP, terms), jnp.int32),
            pltpu.SMEM((slots,), jnp.int32),
            pltpu.SMEM((slots,), jnp.int32),
            pltpu.SMEM((columns,), jnp.int32),
            pltpu.SemaphoreType.DMA((8,)),
            pltpu.SemaphoreType.DMA((6,)),
        ],
        cost_estimate=brief(),
        compiler_params=params(),
        name="load_and_flip",
    )(*[pltpu.with_memory_space_constraint(array, pltpu.HBM) for array in operands])


def pick(pair, layer):
    return jnp.where(layer == 0, pair[0], pair[1])


def ladder_kernel(bits, keeps, sends, parts, waits, *refs):
    table = refs[0]
    amp_parts = refs[1 : 1 + parts]
    tiles, flipped = refs[1 + parts : 3 + parts]
    outs, amps = refs[3 + parts + waits : -1], refs[-1]
    terms = table.shape[1]
    layer = lax.axis_index("layer")
    amp_dev = amp_parts[0].shape[0]
    if parts == 1:
        amps[...] = amp_parts[0][...]
    else:
        row = lax.axis_index("row")
        amps[pl.ds(row * amp_dev, amp_dev)] = amp_parts[0][...]
        amps[pl.ds((1 - row) * amp_dev, amp_dev)] = amp_parts[1][...]
    mask = (1 << bits) - 1
    picked = [(outs[0], i, pick(slots, layer)) for i, slots in enumerate(keeps)]
    picked += [(outs[-1], i, pick(slots, 1 - layer)) for i, slots in enumerate(sends)]
    for out, i, slot in picked:
        lefts, middles = [], []
        for t in range(terms):
            word = table[slot, t]
            lefts.append(tiles[(word >> bits) & mask])
            middles.append(
                jnp.dot(
                    amps[word >> (2 * bits)], flipped[word & mask], preferred_element_type=F32
                ).astype(BF16)
            )
        out[i] = jnp.dot(
            jnp.concatenate(lefts, axis=1),
            jnp.concatenate(middles, axis=0),
            preferred_element_type=F32,
        ).astype(out.dtype)


def merge_kernel(pairs, first, kept, received, label_blocks, *packs):
    edge = kept.shape[1]
    layer = lax.axis_index("layer")
    for i, (pair, packed) in enumerate(zip(pairs, packs)):
        for rank in range(CAP):
            tile = i * CAP + rank
            total = kept[tile] + received[first * CAP + tile]
            packed[rank * edge : (rank + 1) * edge] = total.astype(BF16)
        packed[CAP * edge :] = label_blocks[pick(pair, layer)].astype(BF16)


def late_merge_kernel(offset, kept_at, received_at, kept, received, label_blocks, packed):
    edge = kept.shape[1]
    spot = pl.ds(pl.multiple_of(lax.axis_index("layer") * LABEL_ROWS, LABEL_ROWS), LABEL_ROWS)
    labels = label_blocks[offset, spot, :]
    packed[:edge] = (kept[kept_at] + received[received_at]).astype(BF16)
    packed[edge:] = jnp.concatenate([labels] * CAP, axis=0).astype(BF16)


def join_kernel(*refs):
    joined = refs[-1]
    start = 0
    for part in refs[:-1]:
        joined[start : start + part.shape[0]] = part[...]
        start += part.shape[0]


def pieces(packs, rows, edge):
    for pack in packs:
        ranks = pack.shape[0] // edge
        marks = pack[ranks * edge :, :].astype(F32)
        for rank in range(ranks):
            mark = marks[rank * LABEL_ROWS : (rank + 1) * LABEL_ROWS].reshape(1, LABEL_ROWS, edge)
            tile = pack[pl.ds(rank * edge + rows.start, rows.size), :].astype(F32)
            yield mark, tile.reshape(rows.size // LABEL_ROWS, LABEL_ROWS, edge)


def add_owned(total, parts, s):
    for mark, tile in parts:
        term = jnp.where(mark == s, tile, 0.0)
        total = term if total is None else total + term
    return total


def parts_of(joined, sizes):
    starts = [sum(sizes[:i]) for i in range(len(sizes))]
    return [joined.at[pl.ds(start, size)] for start, size in zip(starts, sizes)]


def near_owner_kernel(sizes, near, out):
    edge = out.shape[2]
    for start in range(0, edge, 32):
        rows = pl.ds(start, 32)
        side = list(pieces(parts_of(near, sizes), rows, edge))
        for s in range(OWN):
            out[s, rows, :] = add_owned(None, side, s).reshape(32, edge)


def last_owner_kernel(sizes, near_sum, far, out, total, sent):
    edge = out.shape[2]
    chunks = sent.shape[0]
    height = edge // chunks

    def copy(i):
        rows = pl.ds(i * height, height)
        return pltpu.make_async_copy(total.at[:, rows, :], out.at[:, rows, :], sent.at[i])

    for i in range(chunks):
        rows = pl.ds(i * height, height)
        side = list(pieces(parts_of(far, sizes), rows, edge))
        for s in range(OWN):
            total[s, rows, :] = near_sum[s, rows, :] + add_owned(None, side, s).reshape(height, edge)
        copy(i).start()
    for i in range(chunks):
        copy(i).wait()


def swap(array, axis):
    size = lax.axis_size(axis)
    return lax.ppermute(array, axis, [(i, i ^ 1) for i in range(size)])


def shards(amplitudes, integrals, amp_index, left_index, right_index, dest_col, owner_slot):
    columns = lax.axis_size("col")
    rows = lax.axis_size("row")
    edge = integrals.shape[1]
    bits = (integrals.shape[0] - 1).bit_length()
    if rows == 2:
        amp_parts = (amplitudes, swap(amplitudes, "row"))
    else:
        amp_parts = (lax.all_gather(amplitudes, "row", axis=0, tiled=True),)
    amp_total = rows * amplitudes.shape[0]
    tiles, flipped, table, label_blocks = prepare(
        columns, bits, integrals, amp_index, left_index, right_index, dest_col.reshape(-1), owner_slot
    )

    def ladder(keeps, sends, after):
        groups = [len(group) for group in (keeps, sends) if group]
        return pl.pallas_call(
            functools.partial(ladder_kernel, bits, keeps, sends, len(amp_parts), len(after)),
            out_shape=tuple(held((slots, edge, edge), F32) for slots in groups),
            in_specs=[smem()] + [vmem()] * (len(amp_parts) + 2) + [pl.BlockSpec(memory_space=pl.ANY)] * len(after),
            out_specs=(vmem(),) * len(groups),
            scratch_shapes=[pltpu.VMEM((amp_total, edge, edge), BF16)],
            cost_estimate=brief(),
            compiler_params=params(),
            name="ladder",
        )(pltpu.with_memory_space_constraint(table, pltpu.SMEM), *[in_vmem(part) for part in amp_parts], in_vmem(tiles), in_vmem(flipped), *after)

    def merge(kernel, rows, count, *arrays):
        return pl.pallas_call(
            kernel,
            out_shape=(held((rows, edge), BF16),) * count,
            in_specs=[vmem()] * len(arrays),
            out_specs=(vmem(),) * count,
            cost_estimate=brief(),
            compiler_params=params(),
            name="merge_layers",
        )(*[in_vmem(array) for array in arrays])

    def join(*packs):
        return pl.pallas_call(
            join_kernel,
            out_shape=held((sum(pack.shape[0] for pack in packs), edge), BF16),
            in_specs=[vmem()] * len(packs),
            out_specs=vmem(),
            cost_estimate=brief(),
            compiler_params=params(),
            name="join_packs",
        )(*[in_vmem(pack) for pack in packs])

    def send(pair, pack):
        route = [
            (layer * columns + c, layer * columns + (c ^ pair[layer])) for layer in range(2) for c in range(columns)
        ]
        return lax.ppermute(pack, ("layer", "col"), route)

    owned = (OWN, edge, edge)

    def near_owner_sum(sizes, near):
        return pl.pallas_call(
            functools.partial(near_owner_kernel, sizes),
            out_shape=held(owned, F32),
            in_specs=[vmem()],
            out_specs=vmem(),
            cost_estimate=brief(),
            compiler_params=params(),
            name="near_owner_sum",
        )(in_vmem(near))

    def last_owner_sum(sizes, *arrays):
        return pl.pallas_call(
            functools.partial(last_owner_kernel, sizes),
            out_shape=jax.ShapeDtypeStruct(owned, F32),
            in_specs=[vmem()] * len(arrays),
            out_specs=pl.BlockSpec(memory_space=pl.ANY),
            scratch_shapes=[pltpu.VMEM(owned, F32), pltpu.SemaphoreType.DMA((4,))],
            cost_estimate=brief(),
            compiler_params=params(),
            name="last_owner_sum",
        )(*[in_vmem(array) for array in arrays])

    pairs = [(d, d - 1) for d in range(columns - 1, 2, -2)]
    slots = sum([round_slots(pair) for pair in pairs], [])
    neighbour, local = late_slots()
    split = len(slots) - CAP
    pair_rows, late_rows = CAP * (edge + LABEL_ROWS), edge + CAP * LABEL_ROWS

    def merge_pairs(first, group, kept):
        kernel = functools.partial(merge_kernel, group, first)
        return merge(kernel, pair_rows, len(group), kept, received, label_blocks)

    def merge_late(offset, kept_at, kept):
        kernel = functools.partial(late_merge_kernel, offset, kept_at, len(slots) + 1 - offset)
        return merge(kernel, late_rows, 1, kept, received, label_blocks)

    (sent,) = ladder([], slots + [neighbour, local], [])
    received = swap(sent, "layer")
    (kept,) = ladder(slots[:split], [], [sent])
    packs = merge_pairs(0, pairs[:-1], kept)
    near = [send(pair, pack) for pair, pack in zip(pairs, packs)]
    (kept,) = ladder(slots[split:] + [neighbour], [], packs)
    packs = merge_pairs(len(pairs) - 1, pairs[-1:], kept) + merge_late(1, CAP, kept)
    near += [send(pair, pack) for pair, pack in zip([pairs[-1], (1, 1)], packs)]
    (kept,) = ladder([local], [], packs)
    near += merge_late(0, 0, kept)

    sizes = [pack.shape[0] for pack in near]
    joined = join(*near)
    return last_owner_sum(sizes, near_owner_sum(sizes, joined), swap(joined, "layer"))


def solution(mesh):
    placed = (
        P(("row", "col"), None, None),
        P(("layer", "row", "col"), None, None),
        P(("layer", "row", "col"), None),
        P(("layer", "row", "col"), None),
        P(("layer", "row", "col"), None),
        P(("row", "col"), None),
        P(("row", "col")),
    )
    return jax.shard_map(
        shards, mesh=mesh, in_specs=placed, out_specs=P(("row", "col"), None, None), check_vma=False
    )
```

```python
import functools

import jax
import jax.numpy as jnp
from jax import lax
from jax.experimental import pallas as pl
from jax.experimental.pallas import tpu as pltpu
from jax.sharding import PartitionSpec as P

OWN = 8
CAP = 2
LABEL_ROWS = 8
F32 = jnp.float32
BF16 = jnp.bfloat16
VMEM_BYTES = 24 << 20


def smem():
    return pl.BlockSpec(memory_space=pltpu.SMEM)


def vmem():
    return pl.BlockSpec(memory_space=pltpu.VMEM)


def held(shape, dtype):
    return pltpu.VMEM(shape, dtype)


def in_vmem(array):
    return pltpu.with_memory_space_constraint(array, pltpu.VMEM)


def params():
    return pltpu.CompilerParams(vmem_limit_bytes=VMEM_BYTES)


def brief():
    return pl.CostEstimate(flops=1 << 20, bytes_accessed=1 << 10, transcendentals=0)


def round_slots(pair):
    return [tuple(offset * CAP + rank for offset in pair) for rank in range(CAP)]


def prepare_kernel(
    bits, source, amp_ids, left_ids, right_ids, dest_in, labels_in,
    tiles, flipped, table, label_blocks, ids, packed, sorted_ids, dest, labels, seen, arrived, ready,
):
    count = tiles.shape[0]
    chunks = arrived.shape[0]
    step = count // chunks
    columns = label_blocks.shape[0]
    small = [
        pltpu.make_async_copy(src, dst, ready.at[i])
        for i, (src, dst) in enumerate(
            [(dest_in, dest), (labels_in, labels)]
            + [(src, ids.at[i]) for i, src in enumerate((amp_ids, left_ids, right_ids))]
        )
    ]

    def copy(i):
        span = pl.ds(i * step, step)
        return pltpu.make_async_copy(source.at[span], tiles.at[span], arrived.at[i])

    for transfer in small:
        transfer.start()
    for i in range(chunks):
        copy(i).start()

    sorted_ids[...] = jnp.zeros(sorted_ids.shape, jnp.int32)
    label_blocks[...] = jnp.full(label_blocks.shape, OWN, F32)
    for d in range(columns):
        seen[d] = 0

    def flip(i):
        copy(i).wait()
        for j in range(step):
            flipped[i * step + j] = tiles[i * step + j].T

    for i in range(chunks // 2):
        flip(i)

    me = lax.axis_index("col")
    for transfer in small:
        transfer.wait()
    packed[...] = (ids[0] << (2 * bits)) | (ids[1] << bits) | ids[2]
    for k in range(packed.shape[0]):
        offset = dest[k] ^ me
        rank = seen[offset]
        seen[offset] = rank + 1
        sorted_ids[pl.ds(offset * CAP + rank, 1), :] = packed[pl.ds(k, 1), :]
        spot = pl.ds(pl.multiple_of(rank * LABEL_ROWS, LABEL_ROWS), LABEL_ROWS)
        label_blocks[offset, spot, :] = jnp.full((LABEL_ROWS, label_blocks.shape[2]), labels[k].astype(F32))
    publish = pltpu.make_async_copy(sorted_ids, table, ready.at[len(small)])
    publish.start()

    for i in range(chunks // 2, chunks):
        flip(i)
    publish.wait()


def prepare(columns, bits, integrals, amp_index, left_index, right_index, target, owner_slot):
    shape = integrals.shape
    slots, terms = amp_index.shape
    operands = (integrals, amp_index, left_index, right_index, target, owner_slot)
    return pl.pallas_call(
        functools.partial(prepare_kernel, bits),
        out_shape=(
            held(shape, BF16),
            held(shape, BF16),
            pltpu.SMEM((columns * CAP, terms), jnp.int32),
            held((columns, CAP * LABEL_ROWS, shape[2]), F32),
        ),
        in_specs=[pl.BlockSpec(memory_space=pltpu.HBM)] * len(operands),
        out_specs=(vmem(), vmem(), smem(), vmem()),
        scratch_shapes=[
            pltpu.VMEM((3, slots, terms), jnp.int32),
            pltpu.VMEM((slots, terms), jnp.int32),
            pltpu.VMEM((columns * CAP, terms), jnp.int32),
            pltpu.SMEM((slots,), jnp.int32),
            pltpu.SMEM((slots,), jnp.int32),
            pltpu.SMEM((columns,), jnp.int32),
            pltpu.SemaphoreType.DMA((8,)),
            pltpu.SemaphoreType.DMA((6,)),
        ],
        cost_estimate=brief(),
        compiler_params=params(),
        name="load_and_flip",
    )(*[pltpu.with_memory_space_constraint(array, pltpu.HBM) for array in operands])


def pick(pair, layer):
    return jnp.where(layer == 0, pair[0], pair[1])


def ladder_kernel(bits, keeps, sends, parts, waits, *refs):
    table = refs[0]
    amp_parts = refs[1 : 1 + parts]
    tiles, flipped = refs[1 + parts : 3 + parts]
    outs, amps = refs[3 + parts + waits : -1], refs[-1]
    terms = table.shape[1]
    layer = lax.axis_index("layer")
    amp_dev = amp_parts[0].shape[0]
    if parts == 1:
        amps[...] = amp_parts[0][...]
    else:
        row = lax.axis_index("row")
        amps[pl.ds(row * amp_dev, amp_dev)] = amp_parts[0][...]
        amps[pl.ds((1 - row) * amp_dev, amp_dev)] = amp_parts[1][...]
    mask = (1 << bits) - 1
    picked = [(outs[0], i, pick(slots, layer)) for i, slots in enumerate(keeps)]
    picked += [(outs[-1], i, pick(slots, 1 - layer)) for i, slots in enumerate(sends)]
    for out, i, slot in picked:
        lefts, middles = [], []
        for t in range(terms):
            word = table[slot, t]
            lefts.append(tiles[(word >> bits) & mask])
            middles.append(
                jnp.dot(
                    amps[word >> (2 * bits)], flipped[word & mask], preferred_element_type=F32
                ).astype(BF16)
            )
        out[i] = jnp.dot(
            jnp.concatenate(lefts, axis=1),
            jnp.concatenate(middles, axis=0),
            preferred_element_type=F32,
        ).astype(out.dtype)


def merge_kernel(pairs, first, kept, received, label_blocks, *packs):
    edge = kept.shape[1]
    layer = lax.axis_index("layer")
    for i, (pair, packed) in enumerate(zip(pairs, packs)):
        for rank in range(CAP):
            tile = i * CAP + rank
            total = kept[tile] + received[first * CAP + tile]
            packed[rank * edge : (rank + 1) * edge] = total.astype(BF16)
        packed[CAP * edge :] = label_blocks[pick(pair, layer)].astype(BF16)


def neighbour_merge_kernel(kept_at, received_at, kept, received, label_blocks, packed):
    edge = kept.shape[1]
    spot = pl.ds(pl.multiple_of(lax.axis_index("layer") * LABEL_ROWS, LABEL_ROWS), LABEL_ROWS)
    labels = label_blocks[1, spot, :]
    packed[:edge] = (kept[kept_at] + received[received_at]).astype(BF16)
    packed[edge:] = jnp.concatenate([labels] * CAP, axis=0).astype(BF16)


def local_kernel(kept, label_blocks, packed):
    edge = kept.shape[1]
    for rank in range(CAP):
        packed[rank * edge : (rank + 1) * edge] = kept[rank].astype(BF16)
    packed[CAP * edge :] = label_blocks[0].astype(BF16)


def join_kernel(*refs):
    joined = refs[-1]
    start = 0
    for part in refs[:-1]:
        joined[start : start + part.shape[0]] = part[...]
        start += part.shape[0]


def pieces(packs, rows, edge):
    for pack in packs:
        ranks = pack.shape[0] // edge
        marks = pack[ranks * edge :, :].astype(F32)
        for rank in range(ranks):
            mark = marks[rank * LABEL_ROWS : (rank + 1) * LABEL_ROWS].reshape(1, LABEL_ROWS, edge)
            tile = pack[pl.ds(rank * edge + rows.start, rows.size), :].astype(F32)
            yield mark, tile.reshape(rows.size // LABEL_ROWS, LABEL_ROWS, edge)


def add_owned(total, parts, s):
    for mark, tile in parts:
        term = jnp.where(mark == s, tile, 0.0)
        total = term if total is None else total + term
    return total


def parts_of(joined, sizes):
    starts = [sum(sizes[:i]) for i in range(len(sizes))]
    return [joined.at[pl.ds(start, size)] for start, size in zip(starts, sizes)]


def near_owner_kernel(sizes, near, out):
    edge = out.shape[2]
    for start in range(0, edge, 32):
        rows = pl.ds(start, 32)
        side = list(pieces(parts_of(near, sizes), rows, edge))
        for s in range(OWN):
            out[s, rows, :] = add_owned(None, side, s).reshape(32, edge)


def last_owner_kernel(sizes, near_sum, far, out, total, sent):
    edge = out.shape[2]
    chunks = sent.shape[0]
    height = edge // chunks

    def copy(i):
        rows = pl.ds(i * height, height)
        return pltpu.make_async_copy(total.at[:, rows, :], out.at[:, rows, :], sent.at[i])

    for i in range(chunks):
        rows = pl.ds(i * height, height)
        side = list(pieces(parts_of(far, sizes), rows, edge))
        for s in range(OWN):
            total[s, rows, :] = near_sum[s, rows, :] + add_owned(None, side, s).reshape(height, edge)
        copy(i).start()
    for i in range(chunks):
        copy(i).wait()


def swap(array, axis):
    size = lax.axis_size(axis)
    return lax.ppermute(array, axis, [(i, i ^ 1) for i in range(size)])


def shards(amplitudes, integrals, amp_index, left_index, right_index, dest_col, owner_slot):
    columns = lax.axis_size("col")
    rows = lax.axis_size("row")
    edge = integrals.shape[1]
    bits = (integrals.shape[0] - 1).bit_length()
    if rows == 2:
        amp_parts = (amplitudes, swap(amplitudes, "row"))
    else:
        amp_parts = (lax.all_gather(amplitudes, "row", axis=0, tiled=True),)
    amp_total = rows * amplitudes.shape[0]
    tiles, flipped, table, label_blocks = prepare(
        columns, bits, integrals, amp_index, left_index, right_index, dest_col.reshape(-1), owner_slot
    )

    def ladder(keeps, sends, after):
        groups = [len(group) for group in (keeps, sends) if group]
        return pl.pallas_call(
            functools.partial(ladder_kernel, bits, keeps, sends, len(amp_parts), len(after)),
            out_shape=tuple(held((slots, edge, edge), F32) for slots in groups),
            in_specs=[smem()] + [vmem()] * (len(amp_parts) + 2) + [pl.BlockSpec(memory_space=pl.ANY)] * len(after),
            out_specs=(vmem(),) * len(groups),
            scratch_shapes=[pltpu.VMEM((amp_total, edge, edge), BF16)],
            cost_estimate=brief(),
            compiler_params=params(),
            name="ladder",
        )(pltpu.with_memory_space_constraint(table, pltpu.SMEM), *[in_vmem(part) for part in amp_parts], in_vmem(tiles), in_vmem(flipped), *after)

    def merge(kernel, rows, count, *arrays):
        return pl.pallas_call(
            kernel,
            out_shape=(held((rows, edge), BF16),) * count,
            in_specs=[vmem()] * len(arrays),
            out_specs=(vmem(),) * count,
            cost_estimate=brief(),
            compiler_params=params(),
            name="merge_layers",
        )(*[in_vmem(array) for array in arrays])

    def join(*packs):
        return pl.pallas_call(
            join_kernel,
            out_shape=held((sum(pack.shape[0] for pack in packs), edge), BF16),
            in_specs=[vmem()] * len(packs),
            out_specs=vmem(),
            cost_estimate=brief(),
            compiler_params=params(),
            name="join_packs",
        )(*[in_vmem(pack) for pack in packs])

    def send(pair, pack):
        route = [
            (layer * columns + c, layer * columns + (c ^ pair[layer])) for layer in range(2) for c in range(columns)
        ]
        return lax.ppermute(pack, ("layer", "col"), route)

    owned = (OWN, edge, edge)

    def near_owner_sum(sizes, near):
        return pl.pallas_call(
            functools.partial(near_owner_kernel, sizes),
            out_shape=held(owned, F32),
            in_specs=[vmem()],
            out_specs=vmem(),
            cost_estimate=brief(),
            compiler_params=params(),
            name="near_owner_sum",
        )(in_vmem(near))

    def last_owner_sum(sizes, *arrays):
        return pl.pallas_call(
            functools.partial(last_owner_kernel, sizes),
            out_shape=jax.ShapeDtypeStruct(owned, F32),
            in_specs=[vmem()] * len(arrays),
            out_specs=pl.BlockSpec(memory_space=pl.ANY),
            scratch_shapes=[pltpu.VMEM(owned, F32), pltpu.SemaphoreType.DMA((4,))],
            cost_estimate=brief(),
            compiler_params=params(),
            name="last_owner_sum",
        )(*[in_vmem(array) for array in arrays])

    pairs = [(d - 1, d) for d in range(columns - 1, 2, -2)]
    slots = sum([round_slots(pair) for pair in pairs], [])
    neighbour = tuple(CAP + rank for rank in range(CAP))
    split = len(slots) - CAP
    pair_rows, half_rows = CAP * (edge + LABEL_ROWS), edge + CAP * LABEL_ROWS

    def merge_pairs(first, group, kept):
        kernel = functools.partial(merge_kernel, group, first)
        return merge(kernel, pair_rows, len(group), kept, received, label_blocks)

    (sent,) = ladder([], slots + [neighbour], [])
    received = swap(sent, "layer")
    (kept,) = ladder(slots[:split], [], [sent])
    packs = merge_pairs(0, pairs[:-1], kept)
    near = [send(pair, pack) for pair, pack in zip(pairs, packs)]

    (kept,) = ladder(slots[split:] + [neighbour], [], packs)
    kernel = functools.partial(neighbour_merge_kernel, CAP, len(slots))
    packs = merge_pairs(len(pairs) - 1, pairs[-1:], kept)
    packs += merge(kernel, half_rows, 1, kept, received, label_blocks)
    near += [send(pair, pack) for pair, pack in zip([pairs[-1], (1, 1)], packs)]

    (kept,) = ladder(round_slots((0, 0)), [], packs)
    near += merge(local_kernel, pair_rows, 1, kept, label_blocks)

    sizes = [pack.shape[0] for pack in near]
    joined = join(*near)
    return last_owner_sum(sizes, near_owner_sum(sizes, joined), swap(joined, "layer"))


def solution(mesh):
    placed = (
        P(("row", "col"), None, None),
        P(("layer", "row", "col"), None, None),
        P(("layer", "row", "col"), None),
        P(("layer", "row", "col"), None),
        P(("layer", "row", "col"), None),
        P(("row", "col"), None),
        P(("row", "col")),
    )
    return jax.shard_map(
        shards, mesh=mesh, in_specs=placed, out_specs=P(("row", "col"), None, None), check_vma=False
    )
```

```python
import functools

import jax
import jax.numpy as jnp
from jax import lax
from jax.experimental import pallas as pl
from jax.experimental.pallas import tpu as pltpu
from jax.sharding import PartitionSpec as P

OWN = 8
CAP = 2
LABEL_ROWS = 8
F32 = jnp.float32
BF16 = jnp.bfloat16
VMEM_BYTES = 24 << 20


def smem():
    return pl.BlockSpec(memory_space=pltpu.SMEM)


def vmem():
    return pl.BlockSpec(memory_space=pltpu.VMEM)


def held(shape, dtype):
    return pltpu.VMEM(shape, dtype)


def in_vmem(array):
    return pltpu.with_memory_space_constraint(array, pltpu.VMEM)


def params():
    return pltpu.CompilerParams(vmem_limit_bytes=VMEM_BYTES)


def brief():
    return pl.CostEstimate(flops=1 << 20, bytes_accessed=1 << 10, transcendentals=0)


def round_slots(pair):
    return [tuple(offset * CAP + rank for offset in pair) for rank in range(CAP)]


def prepare_kernel(
    bits, source, amp_ids, left_ids, right_ids, dest_in, labels_in,
    tiles, flipped, table, label_blocks, ids, packed, sorted_ids, dest, labels, seen, arrived, ready,
):
    count = tiles.shape[0]
    chunks = arrived.shape[0]
    step = count // chunks
    columns = label_blocks.shape[0]
    small = [
        pltpu.make_async_copy(src, dst, ready.at[i])
        for i, (src, dst) in enumerate(
            [(dest_in, dest), (labels_in, labels)]
            + [(src, ids.at[i]) for i, src in enumerate((amp_ids, left_ids, right_ids))]
        )
    ]

    def copy(i):
        span = pl.ds(i * step, step)
        return pltpu.make_async_copy(source.at[span], tiles.at[span], arrived.at[i])

    for transfer in small:
        transfer.start()
    for i in range(chunks):
        copy(i).start()

    sorted_ids[...] = jnp.zeros(sorted_ids.shape, jnp.int32)
    label_blocks[...] = jnp.full(label_blocks.shape, OWN, F32)
    for d in range(columns):
        seen[d] = 0

    def flip(i):
        copy(i).wait()
        for j in range(step):
            flipped[i * step + j] = tiles[i * step + j].T

    for i in range(chunks // 2):
        flip(i)

    me = lax.axis_index("col")
    for transfer in small:
        transfer.wait()
    packed[...] = (ids[0] << (2 * bits)) | (ids[1] << bits) | ids[2]
    for k in range(packed.shape[0]):
        offset = dest[k] ^ me
        rank = seen[offset]
        seen[offset] = rank + 1
        sorted_ids[pl.ds(offset * CAP + rank, 1), :] = packed[pl.ds(k, 1), :]
        spot = pl.ds(pl.multiple_of(rank * LABEL_ROWS, LABEL_ROWS), LABEL_ROWS)
        label_blocks[offset, spot, :] = jnp.full((LABEL_ROWS, label_blocks.shape[2]), labels[k].astype(F32))
    publish = pltpu.make_async_copy(sorted_ids, table, ready.at[len(small)])
    publish.start()

    for i in range(chunks // 2, chunks):
        flip(i)
    publish.wait()


def prepare(columns, bits, integrals, amp_index, left_index, right_index, target, owner_slot):
    shape = integrals.shape
    slots, terms = amp_index.shape
    operands = (integrals, amp_index, left_index, right_index, target, owner_slot)
    return pl.pallas_call(
        functools.partial(prepare_kernel, bits),
        out_shape=(
            held(shape, BF16),
            held(shape, BF16),
            pltpu.SMEM((columns * CAP, terms), jnp.int32),
            held((columns, CAP * LABEL_ROWS, shape[2]), F32),
        ),
        in_specs=[pl.BlockSpec(memory_space=pltpu.HBM)] * len(operands),
        out_specs=(vmem(), vmem(), smem(), vmem()),
        scratch_shapes=[
            pltpu.VMEM((3, slots, terms), jnp.int32),
            pltpu.VMEM((slots, terms), jnp.int32),
            pltpu.VMEM((columns * CAP, terms), jnp.int32),
            pltpu.SMEM((slots,), jnp.int32),
            pltpu.SMEM((slots,), jnp.int32),
            pltpu.SMEM((columns,), jnp.int32),
            pltpu.SemaphoreType.DMA((8,)),
            pltpu.SemaphoreType.DMA((6,)),
        ],
        cost_estimate=brief(),
        compiler_params=params(),
        name="load_and_flip",
    )(*[pltpu.with_memory_space_constraint(array, pltpu.HBM) for array in operands])


def pick(pair, layer):
    return jnp.where(layer == 0, pair[0], pair[1])


def ladder_kernel(bits, keeps, sends, parts, waits, *refs):
    table = refs[0]
    amp_parts = refs[1 : 1 + parts]
    tiles, flipped = refs[1 + parts : 3 + parts]
    outs, amps = refs[3 + parts + waits : -1], refs[-1]
    terms = table.shape[1]
    layer = lax.axis_index("layer")
    amp_dev = amp_parts[0].shape[0]
    if parts == 1:
        amps[...] = amp_parts[0][...]
    else:
        row = lax.axis_index("row")
        amps[pl.ds(row * amp_dev, amp_dev)] = amp_parts[0][...]
        amps[pl.ds((1 - row) * amp_dev, amp_dev)] = amp_parts[1][...]
    mask = (1 << bits) - 1
    picked = [(outs[0], i, pick(slots, layer)) for i, slots in enumerate(keeps)]
    picked += [(outs[-1], i, pick(slots, 1 - layer)) for i, slots in enumerate(sends)]
    for out, i, slot in picked:
        lefts, middles = [], []
        for t in range(terms):
            word = table[slot, t]
            lefts.append(tiles[(word >> bits) & mask])
            middles.append(
                jnp.dot(
                    amps[word >> (2 * bits)], flipped[word & mask], preferred_element_type=F32
                ).astype(BF16)
            )
        out[i] = jnp.dot(
            jnp.concatenate(lefts, axis=1),
            jnp.concatenate(middles, axis=0),
            preferred_element_type=F32,
        ).astype(out.dtype)


def merge_kernel(pairs, first, kept, received, label_blocks, *packs):
    edge = kept.shape[1]
    layer = lax.axis_index("layer")
    for i, (pair, packed) in enumerate(zip(pairs, packs)):
        for rank in range(CAP):
            tile = i * CAP + rank
            total = kept[tile] + received[first * CAP + tile]
            packed[rank * edge : (rank + 1) * edge] = total.astype(BF16)
        packed[CAP * edge :] = label_blocks[pick(pair, layer)].astype(BF16)


def neighbour_merge_kernel(kept_at, received_at, kept, received, label_blocks, packed):
    edge = kept.shape[1]
    spot = pl.ds(pl.multiple_of(lax.axis_index("layer") * LABEL_ROWS, LABEL_ROWS), LABEL_ROWS)
    labels = label_blocks[1, spot, :]
    packed[:edge] = (kept[kept_at] + received[received_at]).astype(BF16)
    packed[edge:] = jnp.concatenate([labels] * CAP, axis=0).astype(BF16)


def local_kernel(kept, label_blocks, packed):
    edge = kept.shape[1]
    for rank in range(CAP):
        packed[rank * edge : (rank + 1) * edge] = kept[rank].astype(BF16)
    packed[CAP * edge :] = label_blocks[0].astype(BF16)


def join_kernel(*refs):
    joined = refs[-1]
    start = 0
    for part in refs[:-1]:
        joined[start : start + part.shape[0]] = part[...]
        start += part.shape[0]


def pieces(packs, rows, edge):
    for pack in packs:
        ranks = pack.shape[0] // edge
        marks = pack[ranks * edge :, :].astype(F32)
        for rank in range(ranks):
            mark = marks[rank * LABEL_ROWS : (rank + 1) * LABEL_ROWS].reshape(1, LABEL_ROWS, edge)
            tile = pack[pl.ds(rank * edge + rows.start, rows.size), :].astype(F32)
            yield mark, tile.reshape(rows.size // LABEL_ROWS, LABEL_ROWS, edge)


def add_owned(total, parts, s):
    for mark, tile in parts:
        term = jnp.where(mark == s, tile, 0.0)
        total = term if total is None else total + term
    return total


def parts_of(joined, sizes):
    starts = [sum(sizes[:i]) for i in range(len(sizes))]
    return [joined.at[pl.ds(start, size)] for start, size in zip(starts, sizes)]


def near_owner_kernel(sizes, near, out):
    edge = out.shape[2]
    for start in range(0, edge, 32):
        rows = pl.ds(start, 32)
        side = list(pieces(parts_of(near, sizes), rows, edge))
        for s in range(OWN):
            out[s, rows, :] = add_owned(None, side, s).reshape(32, edge)


def last_owner_kernel(sizes, near_sum, far, out, total, sent):
    edge = out.shape[2]
    chunks = sent.shape[0]
    height = edge // chunks

    def copy(i):
        rows = pl.ds(i * height, height)
        return pltpu.make_async_copy(total.at[:, rows, :], out.at[:, rows, :], sent.at[i])

    for i in range(chunks):
        rows = pl.ds(i * height, height)
        side = list(pieces(parts_of(far, sizes), rows, edge))
        for s in range(OWN):
            total[s, rows, :] = near_sum[s, rows, :] + add_owned(None, side, s).reshape(height, edge)
        copy(i).start()
    for i in range(chunks):
        copy(i).wait()


def swap(array, axis):
    size = lax.axis_size(axis)
    return lax.ppermute(array, axis, [(i, i ^ 1) for i in range(size)])


def shards(amplitudes, integrals, amp_index, left_index, right_index, dest_col, owner_slot):
    columns = lax.axis_size("col")
    rows = lax.axis_size("row")
    edge = integrals.shape[1]
    bits = (integrals.shape[0] - 1).bit_length()
    if rows == 2:
        amp_parts = (amplitudes, swap(amplitudes, "row"))
    else:
        amp_parts = (lax.all_gather(amplitudes, "row", axis=0, tiled=True),)
    amp_total = rows * amplitudes.shape[0]
    tiles, flipped, table, label_blocks = prepare(
        columns, bits, integrals, amp_index, left_index, right_index, dest_col.reshape(-1), owner_slot
    )

    def ladder(keeps, sends, after):
        groups = [len(group) for group in (keeps, sends) if group]
        return pl.pallas_call(
            functools.partial(ladder_kernel, bits, keeps, sends, len(amp_parts), len(after)),
            out_shape=tuple(held((slots, edge, edge), F32) for slots in groups),
            in_specs=[smem()] + [vmem()] * (len(amp_parts) + 2) + [pl.BlockSpec(memory_space=pl.ANY)] * len(after),
            out_specs=(vmem(),) * len(groups),
            scratch_shapes=[pltpu.VMEM((amp_total, edge, edge), BF16)],
            cost_estimate=brief(),
            compiler_params=params(),
            name="ladder",
        )(pltpu.with_memory_space_constraint(table, pltpu.SMEM), *[in_vmem(part) for part in amp_parts], in_vmem(tiles), in_vmem(flipped), *after)

    def merge(kernel, rows, count, *arrays):
        return pl.pallas_call(
            kernel,
            out_shape=(held((rows, edge), BF16),) * count,
            in_specs=[vmem()] * len(arrays),
            out_specs=(vmem(),) * count,
            cost_estimate=brief(),
            compiler_params=params(),
            name="merge_layers",
        )(*[in_vmem(array) for array in arrays])

    def join(*packs):
        return pl.pallas_call(
            join_kernel,
            out_shape=held((sum(pack.shape[0] for pack in packs), edge), BF16),
            in_specs=[vmem()] * len(packs),
            out_specs=vmem(),
            cost_estimate=brief(),
            compiler_params=params(),
            name="join_packs",
        )(*[in_vmem(pack) for pack in packs])

    def send(pair, pack):
        route = [
            (layer * columns + c, layer * columns + (c ^ pair[layer])) for layer in range(2) for c in range(columns)
        ]
        return lax.ppermute(pack, ("layer", "col"), route)

    owned = (OWN, edge, edge)

    def near_owner_sum(sizes, near):
        return pl.pallas_call(
            functools.partial(near_owner_kernel, sizes),
            out_shape=held(owned, F32),
            in_specs=[vmem()],
            out_specs=vmem(),
            cost_estimate=brief(),
            compiler_params=params(),
            name="near_owner_sum",
        )(in_vmem(near))

    def last_owner_sum(sizes, *arrays):
        return pl.pallas_call(
            functools.partial(last_owner_kernel, sizes),
            out_shape=jax.ShapeDtypeStruct(owned, F32),
            in_specs=[vmem()] * len(arrays),
            out_specs=pl.BlockSpec(memory_space=pl.ANY),
            scratch_shapes=[pltpu.VMEM(owned, F32), pltpu.SemaphoreType.DMA((4,))],
            cost_estimate=brief(),
            compiler_params=params(),
            name="last_owner_sum",
        )(*[in_vmem(array) for array in arrays])

    pairs = [(d - 1, d) for d in range(columns - 1, 2, -2)]
    slots = sum([round_slots(pair) for pair in pairs], [])
    neighbour = tuple(CAP + rank for rank in range(CAP))
    split = len(slots) - CAP
    pair_rows, half_rows = CAP * (edge + LABEL_ROWS), edge + CAP * LABEL_ROWS

    def merge_pairs(first, group, kept):
        kernel = functools.partial(merge_kernel, group, first)
        return merge(kernel, pair_rows, len(group), kept, received, label_blocks)

    (sent,) = ladder([], slots + [neighbour], [])
    received = swap(sent, "layer")
    (kept,) = ladder(slots[:split], [], [sent])
    packs = merge_pairs(0, pairs[:-1], kept)
    near = [send(pair, pack) for pair, pack in zip(pairs, packs)]

    (kept,) = ladder(slots[split:], [], packs)
    packs = merge_pairs(len(pairs) - 1, pairs[-1:], kept)
    (kept,) = ladder([neighbour], [], packs)
    kernel = functools.partial(neighbour_merge_kernel, 0, len(slots))
    packs += merge(kernel, half_rows, 1, kept, received, label_blocks)
    near += [send(pair, pack) for pair, pack in zip([pairs[-1], (1, 1)], packs)]

    (kept,) = ladder(round_slots((0, 0)), [], packs)
    near += merge(local_kernel, pair_rows, 1, kept, label_blocks)

    sizes = [pack.shape[0] for pack in near]
    joined = join(*near)
    return last_owner_sum(sizes, near_owner_sum(sizes, joined), swap(joined, "layer"))


def solution(mesh):
    placed = (
        P(("row", "col"), None, None),
        P(("layer", "row", "col"), None, None),
        P(("layer", "row", "col"), None),
        P(("layer", "row", "col"), None),
        P(("layer", "row", "col"), None),
        P(("row", "col"), None),
        P(("row", "col")),
    )
    return jax.shard_map(
        shards, mesh=mesh, in_specs=placed, out_specs=P(("row", "col"), None, None), check_vma=False
    )
```
